32 devices in a mesh: gx: 4 (over x, core), gy: 2 (over y), gz: 4 (over z).
Axes of the slice: x: 2, y: 2, z: 4, core: 2. Of those that a mesh axis runs over, the one named last changes fastest.
Arguments:
- positions: float32 [3, 4, 2, 4, 32], P(None, 'gx', 'gy', 'gz'), as said below
- species: int32 [4, 2, 4, 32], P('gx', 'gy', 'gz'), may hold values from 0 to 88
- atom_count: int32 [4, 2, 4], P('gx', 'gy', 'gz'), may hold values from 16 to 32, as said below
- edge_count: int32 [4, 2, 4], P('gx', 'gy', 'gz'), may hold values from 0 to 1792, as said below
- sender: int32 [4, 2, 4, 1792], P('gx', 'gy', 'gz'), may hold values from 0 to 863, as said below
- receiver: int32 [4, 2, 4, 1792], P('gx', 'gy', 'gz'), may hold values from 0 to 31, as said below
- image_shift: int32 [3, 4, 2, 4, 1792], P(None, 'gx', 'gy', 'gz'), may hold values from -1 to 1, as said below
- embed: float32 [89, 128], replicated, may hold values from -6 to 6
- radial_in: float32 [2, 8, 64], replicated, may hold values from -2 to 2
- radial_out: float32 [2, 64, 384], replicated, may hold values from -0.75 to 0.75
- w_up: float32 [2, 128, 128], replicated, may hold values from -0.5 to 0.5
- lam: float32 [2, 2, 128], replicated, may hold values from -4 to 4
- w_mix: float32 [2, 128, 128], replicated, may hold values from -0.5 to 0.5
- read_one: float32 [128], replicated, may hold values from -0.5 to 0.5
- read_hidden: float32 [128, 16], replicated, may hold values from -0.5 to 0.5
- read_out: float32 [16], replicated, may hold values from -1.5 to 1.5
Outputs:
- site_energy: float32 [4, 2, 4, 32], P('gx', 'gy', 'gz')
- forces: float32 [3, 4, 2, 4, 32], P(None, 'gx', 'gy', 'gz')
The draws below stay inside these ranges and needn't reach their ends.
Inputs may be any that keep to these rules, and one draw needn't show every extreme that they name: `atom_count`: slots at and above a brick's count are empty: no edge names them, and their species and positions are placeholders. At least one brick is full. `edge_count`: some brick has all 1792 edge slots live. A live edge names an owned slot of the neighbour block; sender and receiver are 0 on edges that are not live. Each live edge's image-shifted sender lies within 5.5 angstrom of its receiver; every pair of owned atoms within 5 angstrom of each other, over all periodic images, is a live edge of the receiver's brick; the (sender image, receiver) pairs within a brick are distinct. A live edge's receiver is below atom_count. `image_shift`: nonzero only where the neighbour block lies across the box's boundary; 0 on edges that are not live. `positions`: any two atoms are at least 1 angstrom apart.
All inputs are finite; a program needn't handle non-finite values.
Results may differ from the reference program's by a relative error of at most 0.0085.
Values may be sent and summed in bfloat16 or wider, within the bound.
A program may use at most 128 MiB of HBM per device.

```python
import jax
import jax.numpy as jnp
import numpy as np
from jax import lax

C = 128
NSPEC = 89
NB = 8
RH = 64
RO = 16
ATOMS_DEV = 32
EDGES_DEV = 1792
BRICKS_X = 4
BRICKS_Y = 2
BRICKS_Z = 4


lattice_step = 2.25


jitter_reach = 0.15


near_table = np.array([[a, b, c] for a in (-2, -1, 0, 1, 2) for b in (-2, -1, 0, 1, 2) for c in (-2, -1, 0, 1, 2) if 0 < a * a + b * b + c * c <= 5], dtype=np.int32)


def structure(key):
    count_x, count_y, count_z = (BRICKS_X, BRICKS_Y, BRICKS_Z)
    atoms = ATOMS_DEV
    depth = atoms // 16
    bricks = count_x * count_y * count_z
    near_total = near_table.shape[0]
    key_count, key_centre, key_order = jax.random.split(key, 3)
    counts = jax.random.randint(key_count, (count_x, count_y, count_z), atoms // 2, atoms + 1)
    centre = jax.random.randint(key_centre, (3,), 0, jnp.array([count_x, count_y, count_z], jnp.int32))
    index_x = jnp.arange(count_x, dtype=jnp.int32)[:, None, None]
    index_y = jnp.arange(count_y, dtype=jnp.int32)[None, :, None]
    index_z = jnp.arange(count_z, dtype=jnp.int32)[None, None, :]

    def nearby(idx, mid, total):
        gap = jnp.mod(idx - mid, total)
        return (gap <= 1) | (gap >= total - 1)
    dense = nearby(index_x, centre[0], count_x) & nearby(index_y, centre[1], count_y) & nearby(index_z, centre[2], count_z)
    counts = jnp.where(dense, atoms, counts).reshape(bricks).astype(jnp.int32)
    scores = jax.random.randint(key_order, (bricks, atoms), 0, 1 << 20) * atoms + jnp.arange(atoms, dtype=jnp.int32)[None, :]
    cell_of_slot = jnp.argsort(scores, axis=1).astype(jnp.int32)
    slot_of_cell = jnp.argsort(cell_of_slot, axis=1).astype(jnp.int32)
    index = jnp.arange(bricks, dtype=jnp.int32)
    brick_x = index // (count_y * count_z)
    brick_y = index // count_z % count_y
    brick_z = index % count_z
    cell_x = cell_of_slot // (4 * depth)
    cell_y = cell_of_slot // depth % 4
    cell_z = cell_of_slot % depth
    lattice = jnp.stack([brick_x[:, None] * 4 + cell_x, brick_y[:, None] * 4 + cell_y, brick_z[:, None] * depth + cell_z])
    brick_len = jnp.array([4, 4, depth], jnp.int32)[:, None, None, None]
    spans = jnp.array([4 * count_x, 4 * count_y, depth * count_z], jnp.int32)[:, None, None, None]
    offsets = jnp.array(near_table).T[:, None, None, :]
    moved = lattice[..., None] + offsets
    step = jnp.floor_divide(moved, brick_len) - jnp.floor_divide(lattice[..., None], brick_len)
    wrapped = jnp.floor_divide(moved, spans)
    inside = moved - wrapped * spans
    near_brick = (inside[0] // 4 * count_y + inside[1] // 4) * count_z + inside[2] // depth
    near_cell = (inside[0] % 4 * 4 + inside[1] % 4) * depth + inside[2] % depth
    near_slot = slot_of_cell[near_brick, near_cell]
    live = (near_slot < counts[near_brick]) & (jnp.arange(atoms, dtype=jnp.int32)[None, :, None] < counts[:, None, None])
    block = (step[0] + 1) * 9 + (step[1] + 1) * 3 + (step[2] + 1)
    senders = (block * atoms + near_slot).reshape(bricks, atoms * near_total)
    receivers = jnp.broadcast_to(jnp.arange(atoms, dtype=jnp.int32)[None, :, None], (bricks, atoms, near_total)).reshape(bricks, atoms * near_total)
    shifts = wrapped.reshape(3, bricks, atoms * near_total)
    live = live.reshape(bricks, atoms * near_total)
    order = jnp.argsort(jnp.where(live, 0, 1) * (atoms * near_total) + jnp.arange(atoms * near_total, dtype=jnp.int32)[None, :], axis=1)
    live_sorted = jnp.take_along_axis(live, order, axis=1)
    senders = jnp.where(live_sorted, jnp.take_along_axis(senders, order, axis=1), 0)
    receivers = jnp.where(live_sorted, jnp.take_along_axis(receivers, order, axis=1), 0)
    shifts = jnp.where(live_sorted[None], jnp.take_along_axis(shifts, order[None], axis=2), 0)
    edge_total = jnp.sum(live_sorted.astype(jnp.int32), axis=1)
    return (counts, lattice, senders, receivers, shifts, edge_total)


def draw_positions(key, part):
    counts, lattice, senders, receivers, shifts, edge_total = structure(key)
    key = jax.random.fold_in(key, 5)
    shape = lattice.shape
    jitter = jitter_reach * jnp.tanh(jax.random.normal(key, shape, jnp.float32))
    coords = (lattice.astype(jnp.float32) + 0.5) * lattice_step + jitter
    return coords.reshape(3, BRICKS_X, BRICKS_Y, BRICKS_Z, ATOMS_DEV).astype(jnp.float32)


def draw_atom_count(key, part):
    counts, lattice, senders, receivers, shifts, edge_total = structure(key)
    return counts.reshape(BRICKS_X, BRICKS_Y, BRICKS_Z)


def draw_edge_count(key, part):
    counts, lattice, senders, receivers, shifts, edge_total = structure(key)
    return edge_total.reshape(BRICKS_X, BRICKS_Y, BRICKS_Z).astype(jnp.int32)


def draw_sender(key, part):
    counts, lattice, senders, receivers, shifts, edge_total = structure(key)
    return senders.reshape(BRICKS_X, BRICKS_Y, BRICKS_Z, EDGES_DEV).astype(jnp.int32)


def draw_receiver(key, part):
    counts, lattice, senders, receivers, shifts, edge_total = structure(key)
    return receivers.reshape(BRICKS_X, BRICKS_Y, BRICKS_Z, EDGES_DEV).astype(jnp.int32)


def draw_image_shift(key, part):
    counts, lattice, senders, receivers, shifts, edge_total = structure(key)
    return shifts.reshape(3, BRICKS_X, BRICKS_Y, BRICKS_Z, EDGES_DEV).astype(jnp.int32)


def place_ends(values, rng, smallest, top_value):
    spot = [jax.random.randint(jax.random.fold_in(rng, axis), (), 0, length) for axis, length in enumerate(values.shape)]
    longest = values.shape.index(max(values.shape))
    next_to = spot[:longest] + [(spot[longest] + 1) % values.shape[longest]] + spot[longest + 1:]
    return values.at[tuple(spot)].set(smallest).at[tuple(next_to)].set(top_value)


def normal_values(stream_key, dims, scale, bound, held_as=jnp.bfloat16):
    return jnp.clip(scale * jax.random.normal(stream_key, dims, jnp.float32), -bound, bound).astype(held_as)


def setup_inputs(seed: int = 0) -> dict:
    arg_keys = jax.random.split(jax.random.key(seed), 17)
    positions = draw_positions(jax.random.fold_in(arg_keys[16], 71), 0)
    species = place_ends(jax.random.randint(arg_keys[1], (BRICKS_X, BRICKS_Y, BRICKS_Z, ATOMS_DEV), 0, NSPEC), jax.random.fold_in(arg_keys[1], 1), 0, NSPEC - 1).astype(jnp.int32)
    atom_count = draw_atom_count(jax.random.fold_in(arg_keys[16], 71), 0)
    edge_count = draw_edge_count(jax.random.fold_in(arg_keys[16], 71), 0)
    sender = draw_sender(jax.random.fold_in(arg_keys[16], 71), 0)
    receiver = draw_receiver(jax.random.fold_in(arg_keys[16], 71), 0)
    image_shift = draw_image_shift(jax.random.fold_in(arg_keys[16], 71), 0)
    embed = normal_values(arg_keys[7], (NSPEC, C), 1.0, 6.0, jnp.float32)
    radial_in = normal_values(arg_keys[8], (2, NB, RH), NB ** -0.5, 2.0, jnp.float32)
    radial_out = normal_values(arg_keys[9], (2, RH, 3 * C), RH ** -0.5, 0.75, jnp.float32)
    w_up = normal_values(arg_keys[10], (2, C, C), C ** -0.5, 0.5, jnp.float32)
    lam = normal_values(arg_keys[11], (2, 2, C), 1.0, 4.0, jnp.float32)
    w_mix = normal_values(arg_keys[12], (2, C, C), C ** -0.5, 0.5, jnp.float32)
    read_one = normal_values(arg_keys[13], (C,), C ** -0.5, 0.5, jnp.float32)
    read_hidden = normal_values(arg_keys[14], (C, RO), C ** -0.5, 0.5, jnp.float32)
    read_out = normal_values(arg_keys[15], (RO,), RO ** -0.5, 1.5, jnp.float32)
    return {"positions": positions, "species": species, "atom_count": atom_count, "edge_count": edge_count, "sender": sender, "receiver": receiver, "image_shift": image_shift, "embed": embed, "radial_in": radial_in, "radial_out": radial_out, "w_up": w_up, "lam": lam, "w_mix": w_mix, "read_one": read_one, "read_hidden": read_hidden, "read_out": read_out}


cutoff_radius = 5.0
lattice_step = 2.25
mean_degree = 8.0

def rounded(value):
    kept = lax.optimization_barrier(value.astype(jnp.bfloat16)).astype(jnp.float32)
    return value + lax.stop_gradient(kept - value)

def embed_rows(embed, kinds):
    table = (kinds[:, None] == jnp.arange(embed.shape[0], dtype=jnp.int32)[None, :]).astype(jnp.float32)
    return jnp.dot(table, embed, precision=lax.Precision.HIGHEST).astype(jnp.bfloat16)

def layer(w_in, w_out, w_lift, weights_sq, w_merge, own_pos, ghost_pos, ghost_h, own_h, sender, receiver, shift_len, valid):
    atoms = own_pos.shape[1]
    width = ghost_h.shape[1]
    rel = (jnp.take(ghost_pos, sender, axis=1) + shift_len - jnp.take(own_pos, receiver, axis=1)) / cutoff_radius
    dist2 = lax.optimization_barrier(jnp.sum(rel * rel, axis=0))
    envelope = jnp.square(jnp.maximum(1.0 - dist2, 0.0)) * valid
    nbasis = w_in.shape[0]
    centres = jnp.arange(nbasis, dtype=jnp.float32) / (nbasis - 1)
    basis = jnp.exp(-jnp.square((dist2[None, :] - centres[:, None]) * nbasis))
    hidden = jax.nn.silu(lax.dot_general(basis, w_in, (((0,), (0,)), ((), ())), precision=lax.Precision.HIGHEST))
    radial = jnp.dot(hidden, w_out, precision=lax.Precision.HIGHEST) * envelope[:, None]
    lifted = jnp.take(jnp.dot(ghost_h, w_lift, precision=lax.Precision.HIGHEST), sender, axis=0)
    xpos, ypos, zpos = (rel[0], rel[1], rel[2])
    harmonics = jnp.stack([jnp.ones_like(xpos), 3.0 ** 0.5 * xpos, 3.0 ** 0.5 * ypos, 3.0 ** 0.5 * zpos, 15.0 ** 0.5 * xpos * ypos, 15.0 ** 0.5 * ypos * zpos, 15.0 ** 0.5 * xpos * zpos, 0.5 * 15.0 ** 0.5 * (xpos * xpos - ypos * ypos), 0.5 * 5.0 ** 0.5 * (2.0 * zpos * zpos - xpos * xpos - ypos * ypos)])
    onehot = (receiver[None, :] == jnp.arange(atoms, dtype=jnp.int32)[:, None]).astype(jnp.float32)
    pooling = onehot[None, :, :] * harmonics[:, None, :] / mean_degree
    base_zero = radial[:, :width] * lifted
    base_one = radial[:, width:2 * width] * lifted
    base_two = radial[:, 2 * width:] * lifted
    scalar = jnp.dot(pooling[0], base_zero, precision=lax.Precision.HIGHEST)
    order_one = jnp.einsum('mae,ec->mac', pooling[1:4], base_one, precision=lax.Precision.HIGHEST)
    order_two = jnp.einsum('mae,ec->mac', pooling[4:], base_two, precision=lax.Precision.HIGHEST)
    first = lax.optimization_barrier(jnp.sum(jnp.square(order_one), axis=0))
    second = lax.optimization_barrier(jnp.sum(jnp.square(order_two), axis=0))
    product = scalar + weights_sq[0] * first + weights_sq[1] * second
    return own_h + jnp.dot(product, w_merge, precision=lax.Precision.HIGHEST)

def readout_two(h_two, read_hidden, read_out):
    inner = jax.nn.silu(jnp.dot(h_two, read_hidden, precision=lax.Precision.HIGHEST))
    return jnp.dot(inner, read_out, precision=lax.Precision.HIGHEST)

def reference(positions, species, atom_count, edge_count, sender, receiver, image_shift, embed, radial_in, radial_out, w_up, lam, w_mix, read_one, read_hidden, read_out):
    bricks = BRICKS_X * BRICKS_Y * BRICKS_Z
    atoms = ATOMS_DEV
    edges = EDGES_DEV
    width = embed.shape[1]
    box = jnp.array([BRICKS_X * 4 * lattice_step, BRICKS_Y * 4 * lattice_step, BRICKS_Z * (atoms // 16) * lattice_step], jnp.float32)
    pos_b = positions.reshape(3, bricks, atoms).transpose(1, 0, 2)
    spec_b = species.reshape(bricks, atoms)
    send_b = sender.reshape(bricks, edges)
    recv_b = receiver.reshape(bricks, edges)
    shift_b = image_shift.reshape(3, bricks, edges).transpose(1, 0, 2).astype(jnp.float32) * box[None, :, None]
    valid_b = (jnp.arange(edges, dtype=jnp.int32)[None, :] < edge_count.reshape(bricks, 1)).astype(jnp.float32)
    mask_b = (jnp.arange(atoms, dtype=jnp.int32)[None, :] < atom_count.reshape(bricks, 1)).astype(jnp.float32)
    index = jnp.arange(bricks, dtype=jnp.int32)
    brick_x = index // (BRICKS_Y * BRICKS_Z)
    brick_y = index // BRICKS_Z % BRICKS_Y
    brick_z = index % BRICKS_Z
    columns = []
    for step_x in (-1, 0, 1):
        for step_y in (-1, 0, 1):
            for step_z in (-1, 0, 1):
                near_x = (brick_x + step_x) % BRICKS_X
                near_y = (brick_y + step_y) % BRICKS_Y
                near_z = (brick_z + step_z) % BRICKS_Z
                columns.append((near_x * BRICKS_Y + near_y) * BRICKS_Z + near_z)
    neighbours = jnp.stack(columns, axis=1).astype(jnp.int32)
    h_zero = lax.optimization_barrier(embed_rows(embed, spec_b.reshape(-1))).astype(jnp.float32).reshape(bricks, atoms, width)

    def total(pos_all):

        def first(brick):
            ghost_pos = pos_all[neighbours[brick]].transpose(1, 0, 2).reshape(3, 27 * atoms)
            ghost_h = h_zero[neighbours[brick]].reshape(27 * atoms, width)
            return layer(radial_in[0], radial_out[0], w_up[0], lam[0], w_mix[0], pos_all[brick], ghost_pos, ghost_h, h_zero[brick], send_b[brick], recv_b[brick], shift_b[brick], valid_b[brick])
        h_one = lax.map(jax.checkpoint(first), index)
        h_kept = rounded(h_one)

        def second(brick):
            ghost_pos = pos_all[neighbours[brick]].transpose(1, 0, 2).reshape(3, 27 * atoms)
            ghost_h = h_kept[neighbours[brick]].reshape(27 * atoms, width)
            return layer(radial_in[1], radial_out[1], w_up[1], lam[1], w_mix[1], pos_all[brick], ghost_pos, ghost_h, h_kept[brick], send_b[brick], recv_b[brick], shift_b[brick], valid_b[brick])
        h_two = lax.map(jax.checkpoint(second), index)
        energy_one = jnp.dot(h_one.reshape(-1, width), read_one, precision=lax.Precision.HIGHEST).reshape(bricks, atoms)
        energy_two = readout_two(h_two.reshape(-1, width), read_hidden, read_out).reshape(bricks, atoms)
        energy = (energy_one + energy_two) * mask_b
        return (jnp.sum(energy), energy)
    gradient, energy = jax.grad(total, has_aux=True)(pos_b)
    site_energy = energy.reshape(BRICKS_X, BRICKS_Y, BRICKS_Z, atoms)
    forces = (-gradient).transpose(1, 0, 2).reshape(3, BRICKS_X, BRICKS_Y, BRICKS_Z, atoms)
    return (site_energy, forces)
```

```python
import functools
import itertools

import jax
import jax.numpy as jnp
from jax import lax
from jax.experimental import pallas as pl
from jax.experimental.pallas import tpu as pltpu
from jax.sharding import PartitionSpec as P

cutoff_radius = 5.0
lattice_step = 2.25
mean_degree = 8.0
F32 = jnp.float32
BF16 = jnp.bfloat16
MESH = pl.DeviceIdType.MESH
CH = 256


def dg(a, b, ca, cb):
    return lax.dot_general(a, b, (((ca,), (cb,)), ((), ())), preferred_element_type=F32)


def split(x):
    hi = x.astype(BF16)
    return hi, (x - hi.astype(F32)).astype(BF16)


def dg3(a, b, ca, cb):
    ah, al = split(a)
    bh, bl = split(b)
    return dg(ah, bh, ca, cb) + (dg(ah, bl, ca, cb) + dg(al, bh, ca, cb))


def parts(x):
    p1 = x.astype(BF16).astype(F32)
    p2 = (x - p1).astype(BF16).astype(F32)
    p3 = x - p1 - p2
    return jnp.concatenate([p1, p2, p3, jnp.zeros_like(x)], axis=0).astype(BF16)


def whole(y):
    return y[0:8] + y[8:16] + y[16:24]


def offsets_of(sizes):
    per_axis = [(-1, 0, 1) if n >= 3 else (-1, 0) if n == 2 else (0,) for n in sizes]
    return list(itertools.product(*per_axis))


def kernel(
    sizes,
    counts,
    pos_ref,
    spec_ref,
    sender_ref,
    receiver_ref,
    shift_ref,
    embed_ref,
    win_ref,
    wout_ref,
    wup_ref,
    lam_ref,
    wmix_ref,
    rone_ref,
    rhid_ref,
    rout_ref,
    energy_ref,
    force_ref,
    own8,
    gpos_in,
    h_own,
    h_in,
    dl_out,
    dl_in,
    dp_out,
    dp_in,
    emb_s,
    ohs,
    ohr,
    pool,
    rad,
    lift,
    base,
    pre_s,
    der,
    dlift,
    rows,
    drow,
    send_sem,
    recv_sem,
):
    atoms = pos_ref.shape[1]
    edges = sender_ref.shape[1]
    nb = win_ref.shape[1]
    rh = win_ref.shape[2]
    width = embed_ref.shape[1]
    nspec = embed_ref.shape[0]
    spad = emb_s.shape[0]
    offs = offsets_of(sizes)
    total = len(offs)
    tiles = dp_out.shape[0]
    ghosts = tiles * 128
    here = offs.index(tuple(0 for _ in sizes))
    me = [lax.axis_index(a) for a in ("gx", "gy", "gz")]

    def device(off, sign):
        return tuple(
            lax.rem(m + (sign * o) % n, n) if o else m for m, o, n in zip(me, off, sizes)
        )

    others = [u for u in range(total) if u != here]

    barrier = pltpu.get_barrier_semaphore()
    for u in others:
        pl.semaphore_signal(barrier, inc=1, device_id=device(offs[u], 1), device_id_type=MESH)

    own8[...] = jnp.zeros_like(own8)
    mine = jnp.concatenate([pos_ref[...], spec_ref[...].astype(F32)], axis=0)
    own8[0:4, :] = jnp.concatenate([mine] * 4, axis=1)
    pl.semaphore_wait(barrier, len(others))

    def copy(phase, u, src, dst, sign):
        return pltpu.make_async_remote_copy(
            src_ref=src,
            dst_ref=dst,
            send_sem=send_sem.at[phase, u],
            recv_sem=recv_sem.at[phase, u],
            device_id=device(offs[u], sign),
            device_id_type=MESH,
        )

    sent = []

    def exchange(phase, source, target, sign):
        started = [copy(phase, u, source(u), target.at[u], sign) for u in others]
        for c in started:
            c.start()
        sent.extend(started)
        return started

    first = exchange(0, lambda u: own8, gpos_in, -1)

    gpos_in[here] = own8[...]
    send_id = sender_ref[...]
    block = jnp.right_shift(send_id, 5)
    slot = send_id - block * 32
    bx = (block >= 9).astype(jnp.int32) + (block >= 18).astype(jnp.int32)
    rest = block - 9 * bx
    by = (rest >= 3).astype(jnp.int32) + (rest >= 6).astype(jnp.int32)
    bz = rest - 3 * by
    flat = jnp.zeros_like(block)
    for d, n in zip((bx, by, bz), sizes):
        if n >= 3:
            flat = flat * 3 + d
        elif n == 2:
            flat = flat * 2 + jnp.where(d == 1, 1, 0)
    ghost_id = flat * 32 + slot
    sub = lax.broadcasted_iota(jnp.int32, (128, CH), 0)
    for e in range(0, edges, CH):
        for t in range(tiles):
            ohs[t * 128 : (t + 1) * 128, e : e + CH] = jnp.where(
                sub == ghost_id[:, e : e + CH] - t * 128, 1.0, 0.0
            ).astype(BF16)
    recv_id = receiver_ref[...]
    near = lax.broadcasted_iota(jnp.int32, (atoms, edges), 0) == recv_id
    ohr[...] = jnp.where(near, 1.0, 0.0).astype(BF16)
    at_recv = whole(dg(parts(own8[...])[:, 0:atoms], ohr[...], 1, 0))
    emb_s[...] = jnp.zeros_like(emb_s)
    emb_s[0:nspec, :] = embed_ref[...]
    emb = emb_s[...].astype(BF16)
    wu_h, wu_l = split(wup_ref[0])
    table = (dg(emb, wu_h, 1, 0) + dg(emb, wu_l, 1, 0)).astype(BF16)
    kind = lax.broadcasted_iota(jnp.int32, (spad, 128), 0).astype(F32)
    own_kind = jnp.where(kind == own8[3:4, :], 1.0, 0.0).astype(BF16)
    h0 = dg(own_kind, emb, 0, 0)[0:atoms]
    valid = lax.broadcasted_iota(jnp.int32, (1, edges), 1) < counts[1]
    atom_row = (lax.broadcasted_iota(jnp.int32, (1, atoms), 1) < counts[0]).astype(F32)
    atom_col = (lax.broadcasted_iota(jnp.int32, (atoms, width), 0) < counts[0]).astype(F32)
    if h_in.shape[0] > total:
        h_in[total:] = jnp.zeros((h_in.shape[0] - total, atoms, width), BF16)
    dp_out[...] = jnp.zeros_like(dp_out)

    for c in first:
        c.wait_recv()

    lane = lax.broadcasted_iota(jnp.int32, (8, 128), 1)
    cols = []
    for t in range(tiles):
        tile = jnp.zeros((8, 128), F32)
        for j in range(4):
            if 4 * t + j < total:
                inside = (lane >= 32 * j) & (lane < 32 * j + 32)
                tile = jnp.where(inside, gpos_in[4 * t + j], tile)
        cols.append(tile)
    gpos = jnp.concatenate(cols, axis=1)
    gkind = jnp.concatenate(
        [jnp.where(kind == c[3:4, :], 1.0, 0.0).astype(BF16) for c in cols], axis=1
    )
    ghost_lift = dg(table, gkind, 0, 0).astype(BF16)
    lhs = jnp.concatenate([ghost_lift, parts(gpos)], axis=0)
    at_send = []
    for e in range(0, edges, CH):
        got = dg(lhs, ohs[:, e : e + CH], 1, 0)
        lift[0, :, e : e + CH] = got[0:width]
        at_send.append(whole(got[width:]))
    at_send = jnp.concatenate(at_send, axis=1)

    def axis(a, n, cells):
        length = n * cells * lattice_step
        moved = at_send[a : a + 1] + shift_ref[a : a + 1].astype(F32) * length
        return (moved - at_recv[a : a + 1]) / cutoff_radius

    x = axis(0, sizes[0], 4)
    y = axis(1, sizes[1], 4)
    z = axis(2, sizes[2], atoms // 16)
    dist2 = x * x + y * y + z * z
    inner = jnp.where(valid, jnp.maximum(1.0 - dist2, 0.0), 0.0)
    env = inner * inner
    s3, s5, s15 = 3.0**0.5, 5.0**0.5, 15.0**0.5
    harm = [
        jnp.ones_like(x),
        s3 * x,
        s3 * y,
        s3 * z,
        s15 * x * y,
        s15 * y * z,
        s15 * x * z,
        0.5 * s15 * (x * x - y * y),
        0.5 * s5 * (2.0 * z * z - x * x - y * y),
    ]
    rows[0:1] = x
    rows[1:2] = y
    rows[2:3] = z
    rows[3:4] = dist2
    rows[4:5] = inner
    for m in range(9):
        rows[8 + m : 9 + m] = harm[m] * (1.0 / mean_degree)
        weight = harm[m] * env * (1.0 / mean_degree)
        pool[atoms * m : atoms * (m + 1), :] = jnp.where(near, weight, 0.0).astype(BF16)

    centres = lax.broadcasted_iota(jnp.int32, (nb, edges), 0).astype(F32) / (nb - 1)

    def basis_of():
        return jnp.exp(-jnp.square((rows[3:4] - centres) * nb))

    def radial(t):
        basis = basis_of()
        bh = basis.astype(BF16).astype(F32)
        bl = basis - bh
        wi = win_ref[t]
        wh = wi.astype(BF16).astype(F32)
        wl = wi - wh
        pre = dg(
            jnp.concatenate([wh, wh, wl, wl], axis=0).astype(BF16),
            jnp.concatenate([bh, bl, bh, bl], axis=0).astype(BF16),
            0,
            0,
        )
        pre_s[t] = pre
        hidden = pre * jax.nn.sigmoid(pre)
        hh, hl = split(hidden)
        oh, ol = split(wout_ref[t])
        left = jnp.concatenate([oh, oh, ol], axis=0)
        right = jnp.concatenate([hh, hl, hh], axis=0)
        for e in range(0, edges, CH):
            rad[t, :, e : e + CH] = dg(left, right[:, e : e + CH], 0, 0)

    def pooled(t):
        for e in range(0, edges, CH):
            up = lift[t, :, e : e + CH]
            for k in range(3):
                base[t, k * width : (k + 1) * width, e : e + CH] = (
                    rad[t, k * width : (k + 1) * width, e : e + CH] * up
                ).astype(BF16)
        a0 = dg(pool[0:atoms], base[t, 0:width], 1, 1)
        a1 = dg(pool[atoms : 4 * atoms], base[t, width : 2 * width], 1, 1)
        a2 = dg(pool[4 * atoms : 9 * atoms], base[t, 2 * width : 3 * width], 1, 1)
        a1 = [a1[atoms * m : atoms * (m + 1)] for m in range(3)]
        a2 = [a2[atoms * m : atoms * (m + 1)] for m in range(5)]
        l0, l1 = lam_ref[t, 0:1], lam_ref[t, 1:2]
        q1 = sum(a * a for a in a1)
        q2 = sum(a * a for a in a2)
        return a0 + l0 * q1 + l1 * q2, a1, a2

    def pulled(t, d_prod, a1, a2):
        l0, l1 = lam_ref[t, 0:1], lam_ref[t, 1:2]
        g1 = 2.0 * l0 * d_prod
        g2 = 2.0 * l1 * d_prod
        d_a = [
            d_prod,
            jnp.concatenate([g1 * a for a in a1], axis=0),
            jnp.concatenate([g2 * a for a in a2], axis=0),
        ]
        d_t = [d.T.astype(BF16) for d in d_a]
        d_a = [d.astype(BF16) for d in d_a]
        span = [(0, 1), (1, 4), (4, 9)]
        for e in range(0, edges, CH):
            up = lift[t, :, e : e + CH]
            d_up = jnp.zeros((width, CH), F32)
            for k, (lo, hi) in enumerate(span):
                d_base = dg(d_t[k], pool[lo * atoms : hi * atoms, e : e + CH], 1, 0)
                d_up = d_up + d_base * rad[t, k * width : (k + 1) * width, e : e + CH]
                der[k * width : (k + 1) * width, e : e + CH] = (d_base * up).astype(BF16)
            if t == 1:
                dlift[:, e : e + CH] = d_up.astype(BF16)
        return d_a

    def edge_rows(t, d_a):
        span = [(0, 1), (1, 4), (4, 9)]
        for e in range(0, edges, CH):
            pick = ohr[:, e : e + CH].astype(F32)
            for k, (lo, hi) in enumerate(span):
                q = dg(d_a[k], base[t, k * width : (k + 1) * width, e : e + CH], 1, 0)
                for m in range(lo, hi):
                    part = q[(m - lo) * atoms : (m - lo + 1) * atoms] * pick
                    line = jnp.sum(part, axis=0, keepdims=True)
                    if t == 1:
                        drow[m : m + 1, e : e + CH] = line
                    else:
                        drow[m : m + 1, e : e + CH] += line
        d_hidden = dg(wout_ref[t].astype(BF16), der[...], 1, 0)
        pre = pre_s[t]
        sig = jax.nn.sigmoid(pre)
        d_pre = d_hidden * (sig * (1.0 + pre * (1.0 - sig)))
        d_basis = dg3(win_ref[t], d_pre, 1, 0)
        gap = rows[3:4] - centres
        slope = jnp.sum(d_basis * basis_of() * gap, axis=0, keepdims=True) * (-2.0 * nb * nb)
        if t == 1:
            drow[9:10] = slope
        else:
            drow[9:10] += slope

    radial(0)
    prod1, a1_one, a2_one = pooled(0)
    h1 = h0 + dg3(prod1, wmix_ref[0], 1, 0)
    h_own[...] = h1.astype(BF16)
    second = exchange(1, lambda u: h_own, h_in, -1)
    h_in[here] = h_own[...]
    rone = jnp.broadcast_to(rone_ref[...], (8, width))
    energy1 = dg3(rone, h1, 1, 1)[0:1]
    radial(1)
    wt_h, wt_l = split(wup_ref[1].T)
    for c in second:
        c.wait_recv()

    feats = h_in[...].reshape(ghosts, width)
    ghost_lift = (dg(wt_h, feats, 1, 1) + dg(wt_l, feats, 1, 1)).astype(BF16)
    for e in range(0, edges, CH):
        lift[1, :, e : e + CH] = dg(ghost_lift, ohs[:, e : e + CH], 1, 0)
    prod2, a1_two, a2_two = pooled(1)
    h2 = h_own[...].astype(F32) + dg3(prod2, wmix_ref[1], 1, 0)
    ro_pre = dg3(rhid_ref[...], h2, 1, 1)
    ro_sig = jax.nn.sigmoid(ro_pre)
    energy2 = jnp.sum(ro_pre * ro_sig * rout_ref[...], axis=0, keepdims=True)
    energy_ref[...] = (energy1 + energy2) * atom_row

    d_ro = rout_ref[...] * atom_row * (ro_sig * (1.0 + ro_pre * (1.0 - ro_sig)))
    d_h2 = dg3(d_ro, rhid_ref[...], 0, 0)
    d_prod2 = dg3(d_h2, wmix_ref[1], 1, 1)
    d_a = pulled(1, d_prod2, a1_two, a2_two)
    for t in range(tiles):
        d_ghost = dg(ohs[t * 128 : (t + 1) * 128], dlift[...], 1, 1)
        for j in range(4):
            if 4 * t + j < total:
                dl_out[4 * t + j] = d_ghost[32 * j : 32 * j + 32].astype(BF16)
    third = exchange(2, lambda u: dl_out.at[u], dl_in, 1)
    dl_in[here] = dl_out[here]
    edge_rows(1, d_a)
    for c in third:
        c.wait_recv()

    gathered = dl_in[0].astype(F32)
    for u in range(1, total):
        gathered = gathered + dl_in[u].astype(F32)
    d_h1 = d_h2 + dg3(gathered, wup_ref[1], 1, 1) + atom_col * rone_ref[...]
    d_prod1 = dg3(d_h1, wmix_ref[0], 1, 1)
    d_a = pulled(0, d_prod1, a1_one, a2_one)
    edge_rows(0, d_a)

    x, y, z, inner = rows[0:1], rows[1:2], rows[2:3], rows[4:5]
    env8 = inner * inner * (1.0 / mean_degree)
    d_env = drow[0:1] * rows[8:9]
    for m in range(1, 9):
        d_env = d_env + drow[m : m + 1] * rows[8 + m : 9 + m]
    d_dist = 2.0 * (drow[9:10] - 2.0 * d_env * inner)
    dh = [drow[m : m + 1] * env8 for m in range(9)]
    d_x = d_dist * x + s3 * dh[1] + s15 * (y * dh[4] + z * dh[6] + x * dh[7]) - s5 * x * dh[8]
    d_y = d_dist * y + s3 * dh[2] + s15 * (x * dh[4] + z * dh[5] - y * dh[7]) - s5 * y * dh[8]
    d_z = d_dist * z + s3 * dh[3] + s15 * (y * dh[5] + x * dh[6]) + 2.0 * s5 * z * dh[8]
    drow[0:1] = d_x / cutoff_radius
    drow[1:2] = d_y / cutoff_radius
    drow[2:3] = d_z / cutoff_radius
    drow[3:8] = jnp.zeros((5, edges), F32)
    d_rel = drow[0:8]
    d_hi = d_rel.astype(BF16).astype(F32)
    both = jnp.concatenate([d_hi, d_rel - d_hi], axis=0).astype(BF16)
    for t in range(tiles):
        back = dg(both, ohs[t * 128 : (t + 1) * 128], 1, 1)
        dp_out[t] = back[0:8] + back[8:16]
    fourth = exchange(3, lambda u: dp_out.at[u // 4], dp_in, 1)
    dp_in[here] = dp_out[here // 4]
    own = dg(both, ohr[...], 1, 1)
    for c in fourth:
        c.wait_recv()
    fold = jnp.zeros((8, 128), F32)
    for u in range(total):
        j = u % 4
        inside = (lane >= 32 * j) & (lane < 32 * j + 32)
        fold = fold + jnp.where(inside, dp_in[u], 0.0)
    fold = fold + pltpu.roll(fold, 64, 1)
    fold = fold + pltpu.roll(fold, 32, 1)
    force = own[0:8] + own[8:16] - fold[:, 0:atoms]
    force_ref[...] = force[0:3]
    for c in sent:
        c.wait_send()


def local(
    sizes,
    positions,
    species,
    atom_count,
    edge_count,
    sender,
    receiver,
    image_shift,
    embed,
    radial_in,
    radial_out,
    w_up,
    lam,
    w_mix,
    read_one,
    read_hidden,
    read_out,
):
    atoms = positions.shape[-1]
    edges = sender.shape[-1]
    nspec, width = embed.shape
    rh = radial_in.shape[2]
    total = len(offsets_of(sizes))
    tiles = (total + 3) // 4
    ghosts = tiles * 128
    counts = jnp.concatenate([atom_count.reshape(1), edge_count.reshape(1)])
    vmem = pl.BlockSpec(memory_space=pltpu.VMEM)
    energy, force = pl.pallas_call(
        functools.partial(kernel, sizes),
        out_shape=(
            jax.ShapeDtypeStruct((1, atoms), F32),
            jax.ShapeDtypeStruct((3, atoms), F32),
        ),
        in_specs=[pl.BlockSpec(memory_space=pltpu.SMEM)] + [vmem] * 14,
        out_specs=(vmem, vmem),
        scratch_shapes=[
            pltpu.VMEM((8, 128), F32),
            pltpu.VMEM((total, 8, 128), F32),
            pltpu.VMEM((atoms, width), BF16),
            pltpu.VMEM((4 * tiles, atoms, width), BF16),
            pltpu.VMEM((total, atoms, width), BF16),
            pltpu.VMEM((total, atoms, width), BF16),
            pltpu.VMEM((tiles, 8, 128), F32),
            pltpu.VMEM((total, 8, 128), F32),
            pltpu.VMEM(((nspec + 15) // 16 * 16, width), F32),
            pltpu.VMEM((ghosts, edges), BF16),
            pltpu.VMEM((atoms, edges), BF16),
            pltpu.VMEM((9 * atoms, edges), BF16),
            pltpu.VMEM((2, 3 * width, edges), F32),
            pltpu.VMEM((2, width, edges), F32),
            pltpu.VMEM((2, 3 * width, edges), BF16),
            pltpu.VMEM((2, rh, edges), F32),
            pltpu.VMEM((3 * width, edges), BF16),
            pltpu.VMEM((width, edges), BF16),
            pltpu.VMEM((24, edges), F32),
            pltpu.VMEM((16, edges), F32),
            pltpu.SemaphoreType.DMA((4, total)),
            pltpu.SemaphoreType.DMA((4, total)),
        ],
        compiler_params=pltpu.CompilerParams(
            collective_id=0, has_side_effects=True, vmem_limit_bytes=50 * 1024 * 1024
        ),
    )(
        counts,
        positions.reshape(3, atoms),
        species.reshape(1, atoms),
        sender.reshape(1, edges),
        receiver.reshape(1, edges),
        image_shift.reshape(3, edges),
        embed,
        radial_in,
        radial_out,
        w_up,
        lam,
        w_mix,
        read_one.reshape(1, width),
        read_hidden.T,
        read_out.reshape(-1, 1),
    )
    return energy.reshape(1, 1, 1, atoms), force.reshape(3, 1, 1, 1, atoms)


def solution(mesh):
    sizes = tuple(mesh.shape[a] for a in ("gx", "gy", "gz"))
    in_specs = (
        P(None, "gx", "gy", "gz", None),
        P("gx", "gy", "gz", None),
        P("gx", "gy", "gz"),
        P("gx", "gy", "gz"),
        P("gx", "gy", "gz", None),
        P("gx", "gy", "gz", None),
        P(None, "gx", "gy", "gz", None),
        P(),
        P(),
        P(),
        P(),
        P(),
        P(),
        P(),
        P(),
        P(),
    )
    out_specs = (P("gx", "gy", "gz", None), P(None, "gx", "gy", "gz", None))
    return jax.shard_map(
        functools.partial(local, sizes),
        mesh=mesh,
        in_specs=in_specs,
        out_specs=out_specs,
        check_vma=False,
    )
```

```python
import functools
import itertools

import jax
import jax.numpy as jnp
from jax import lax
from jax.experimental import pallas as pl
from jax.experimental.pallas import tpu as pltpu
from jax.sharding import PartitionSpec as P

cutoff_radius = 5.0
lattice_step = 2.25
mean_degree = 8.0
F32 = jnp.float32
BF16 = jnp.bfloat16
MESH = pl.DeviceIdType.MESH
CH = 256
INPUTS = 16


def dg(a, b, ca, cb):
    return lax.dot_general(a, b, (((ca,), (cb,)), ((), ())), preferred_element_type=F32)


def split(x):
    hi = x.astype(BF16)
    return hi, (x - hi.astype(F32)).astype(BF16)


def dg3(a, b, ca, cb):
    ah, al = split(a)
    bh, bl = split(b)
    return dg(ah, bh, ca, cb) + (dg(ah, bl, ca, cb) + dg(al, bh, ca, cb))


def parts(x):
    p1 = x.astype(BF16).astype(F32)
    p2 = (x - p1).astype(BF16).astype(F32)
    p3 = x - p1 - p2
    return jnp.concatenate([p1, p2, p3, jnp.zeros_like(x)], axis=0).astype(BF16)


def whole(y):
    return y[0:8] + y[8:16] + y[16:24]


def offsets_of(sizes):
    per_axis = [(-1, 0, 1) if n >= 3 else (-1, 0) if n == 2 else (0,) for n in sizes]
    return list(itertools.product(*per_axis))


def kernel(
    sizes,
    *refs,
):
    hbm = refs[:INPUTS]
    energy_ref, force_ref = refs[INPUTS : INPUTS + 2]
    held = refs[INPUTS + 2 : 2 * INPUTS + 2]
    body(sizes, hbm, energy_ref, force_ref, held, *refs[2 * INPUTS + 2 :])


def body(
    sizes,
    hbm,
    energy_ref,
    force_ref,
    held,
    own8,
    gpos_in,
    h_own,
    h_in,
    dl_out,
    dl_in,
    dp_out,
    dp_in,
    emb_s,
    ohs,
    ohr,
    pool,
    rad,
    lift,
    base,
    pre_s,
    der,
    dlift,
    rows,
    drow,
    in_sem,
    send_sem,
    recv_sem,
):
    (
        pos_ref,
        spec_ref,
        acount_ref,
        ecount_ref,
        sender_ref,
        receiver_ref,
        shift_ref,
        embed_ref,
        win_ref,
        wout_ref,
        wup_ref,
        lam_ref,
        wmix_ref,
        rone_ref,
        rhid_ref,
        rout_ref,
    ) = held
    fetch = [
        pltpu.make_async_copy(src, dst, in_sem.at[i])
        for i, (src, dst) in enumerate(zip(hbm, held))
    ]
    for c in fetch:
        c.start()
    atoms = pos_ref.shape[-1]
    edges = sender_ref.shape[-1]
    nb = win_ref.shape[1]
    rh = win_ref.shape[2]
    width = embed_ref.shape[1]
    nspec = embed_ref.shape[0]
    spad = emb_s.shape[0]
    offs = offsets_of(sizes)
    total = len(offs)
    tiles = dp_out.shape[0]
    ghosts = tiles * 128
    here = offs.index(tuple(0 for _ in sizes))
    me = [lax.axis_index(a) for a in ("gx", "gy", "gz")]

    def device(off, sign):
        return tuple(
            lax.rem(m + (sign * o) % n, n) if o else m for m, o, n in zip(me, off, sizes)
        )

    others = [u for u in range(total) if u != here]

    barrier = pltpu.get_barrier_semaphore()
    for u in others:
        pl.semaphore_signal(barrier, inc=1, device_id=device(offs[u], 1), device_id_type=MESH)

    own8[...] = jnp.zeros_like(own8)
    fetch[0].wait()
    fetch[1].wait()
    mine = jnp.concatenate(
        [pos_ref[a, 0, 0] for a in range(3)] + [spec_ref[0, 0].astype(F32)], axis=0
    )
    own8[0:4, :] = jnp.concatenate([mine] * 4, axis=1)
    pl.semaphore_wait(barrier, len(others))

    def copy(phase, u, src, dst, sign):
        return pltpu.make_async_remote_copy(
            src_ref=src,
            dst_ref=dst,
            send_sem=send_sem.at[phase, u],
            recv_sem=recv_sem.at[phase, u],
            device_id=device(offs[u], sign),
            device_id_type=MESH,
        )

    sent = []

    def exchange(phase, source, target, sign, tile=None):
        started = [
            copy(phase, u, source(u), target.at[u], sign)
            for u in others
            if tile is None or u // 4 == tile
        ]
        for c in started:
            c.start()
        sent.extend(started)
        return started

    first = exchange(0, lambda u: own8, gpos_in, -1)

    gpos_in[here] = own8[...]
    for c in fetch[2:]:
        c.wait()
    send_id = sender_ref[0, 0]
    block = jnp.right_shift(send_id, 5)
    slot = send_id - block * 32
    bx = (block >= 9).astype(jnp.int32) + (block >= 18).astype(jnp.int32)
    rest = block - 9 * bx
    by = (rest >= 3).astype(jnp.int32) + (rest >= 6).astype(jnp.int32)
    bz = rest - 3 * by
    flat = jnp.zeros_like(block)
    for d, n in zip((bx, by, bz), sizes):
        if n >= 3:
            flat = flat * 3 + d
        elif n == 2:
            flat = flat * 2 + jnp.where(d == 1, 1, 0)
    ghost_id = flat * 32 + slot
    sub = lax.broadcasted_iota(jnp.int32, (128, CH), 0)
    for e in range(0, edges, CH):
        for t in range(tiles):
            ohs[t * 128 : (t + 1) * 128, e : e + CH] = jnp.where(
                sub == ghost_id[:, e : e + CH] - t * 128, 1.0, 0.0
            ).astype(BF16)
    recv_id = receiver_ref[0, 0]
    near = lax.broadcasted_iota(jnp.int32, (atoms, edges), 0) == recv_id
    ohr[...] = jnp.where(near, 1.0, 0.0).astype(BF16)
    at_recv = whole(dg(parts(own8[...])[:, 0:atoms], ohr[...], 1, 0))
    emb_s[...] = jnp.zeros_like(emb_s)
    emb_s[0:nspec, :] = embed_ref[...]
    emb = emb_s[...].astype(BF16)
    wu_h, wu_l = split(wup_ref[0])
    table = (dg(emb, wu_h, 1, 0) + dg(emb, wu_l, 1, 0)).astype(BF16)
    kind = lax.broadcasted_iota(jnp.int32, (spad, 128), 0).astype(F32)
    own_kind = jnp.where(kind == own8[3:4, :], 1.0, 0.0).astype(BF16)
    h0 = dg(own_kind, emb, 0, 0)[0:atoms]
    valid = lax.broadcasted_iota(jnp.int32, (1, edges), 1) < ecount_ref[0]
    atom_row = (lax.broadcasted_iota(jnp.int32, (1, atoms), 1) < acount_ref[0]).astype(F32)
    atom_col = (lax.broadcasted_iota(jnp.int32, (atoms, width), 0) < acount_ref[0]).astype(F32)
    if h_in.shape[0] > total:
        h_in[total:] = jnp.zeros((h_in.shape[0] - total, atoms, width), BF16)

    for c in first:
        c.wait_recv()

    lane = lax.broadcasted_iota(jnp.int32, (8, 128), 1)
    cols = []
    for t in range(tiles):
        tile = jnp.zeros((8, 128), F32)
        for j in range(4):
            if 4 * t + j < total:
                inside = (lane >= 32 * j) & (lane < 32 * j + 32)
                tile = jnp.where(inside, gpos_in[4 * t + j], tile)
        cols.append(tile)
    gpos = jnp.concatenate(cols, axis=1)
    gkind = jnp.concatenate(
        [jnp.where(kind == c[3:4, :], 1.0, 0.0).astype(BF16) for c in cols], axis=1
    )
    ghost_lift = dg(table, gkind, 0, 0).astype(BF16)
    lhs = jnp.concatenate([ghost_lift, parts(gpos)], axis=0)
    at_send = []
    for e in range(0, edges, CH):
        got = dg(lhs, ohs[:, e : e + CH], 1, 0)
        lift[0, :, e : e + CH] = got[0:width]
        at_send.append(whole(got[width:]))
    at_send = jnp.concatenate(at_send, axis=1)

    def axis(a, n, cells):
        length = n * cells * lattice_step
        moved = at_send[a : a + 1] + shift_ref[a, 0, 0].astype(F32) * length
        return (moved - at_recv[a : a + 1]) / cutoff_radius

    x = axis(0, sizes[0], 4)
    y = axis(1, sizes[1], 4)
    z = axis(2, sizes[2], atoms // 16)
    dist2 = x * x + y * y + z * z
    inner = jnp.where(valid, jnp.maximum(1.0 - dist2, 0.0), 0.0)
    env = inner * inner
    s3, s5, s15 = 3.0**0.5, 5.0**0.5, 15.0**0.5
    harm = [
        jnp.ones_like(x),
        s3 * x,
        s3 * y,
        s3 * z,
        s15 * x * y,
        s15 * y * z,
        s15 * x * z,
        0.5 * s15 * (x * x - y * y),
        0.5 * s5 * (2.0 * z * z - x * x - y * y),
    ]
    rows[0:1] = x
    rows[1:2] = y
    rows[2:3] = z
    rows[3:4] = dist2
    rows[4:5] = inner
    for m in range(9):
        rows[8 + m : 9 + m] = harm[m] * (1.0 / mean_degree)
        weight = harm[m] * env * (1.0 / mean_degree)
        pool[atoms * m : atoms * (m + 1), :] = jnp.where(near, weight, 0.0).astype(BF16)

    centres = lax.broadcasted_iota(jnp.int32, (nb, edges), 0).astype(F32) / (nb - 1)

    def basis_of():
        return jnp.exp(-jnp.square((rows[3:4] - centres) * nb))

    def radial(t):
        basis = basis_of()
        bh = basis.astype(BF16).astype(F32)
        bl = basis - bh
        wi = win_ref[t]
        wh = wi.astype(BF16).astype(F32)
        wl = wi - wh
        pre = dg(
            jnp.concatenate([wh, wh, wl, wl], axis=0).astype(BF16),
            jnp.concatenate([bh, bl, bh, bl], axis=0).astype(BF16),
            0,
            0,
        )
        pre_s[t] = pre
        hidden = pre * jax.nn.sigmoid(pre)
        hh, hl = split(hidden)
        wo = wout_ref[t]
        oh = wo.astype(BF16).astype(F32)
        left = jnp.concatenate([oh, oh, wo - oh], axis=0).T.astype(BF16)
        right = jnp.concatenate([hh, hl, hh], axis=0)
        for e in range(0, edges, CH):
            rad[t, :, e : e + CH] = dg(left, right[:, e : e + CH], 1, 0)

    def pooled(t):
        for e in range(0, edges, CH):
            up = lift[t, :, e : e + CH]
            for k in range(3):
                base[t, k * width : (k + 1) * width, e : e + CH] = (
                    rad[t, k * width : (k + 1) * width, e : e + CH] * up
                ).astype(BF16)
        a0 = dg(pool[0:atoms], base[t, 0:width], 1, 1)
        a1 = dg(pool[atoms : 4 * atoms], base[t, width : 2 * width], 1, 1)
        a2 = dg(pool[4 * atoms : 9 * atoms], base[t, 2 * width : 3 * width], 1, 1)
        a1 = [a1[atoms * m : atoms * (m + 1)] for m in range(3)]
        a2 = [a2[atoms * m : atoms * (m + 1)] for m in range(5)]
        l0, l1 = lam_ref[t, 0:1], lam_ref[t, 1:2]
        q1 = sum(a * a for a in a1)
        q2 = sum(a * a for a in a2)
        return a0 + l0 * q1 + l1 * q2, a1, a2

    def pulled(t, d_prod, a1, a2):
        l0, l1 = lam_ref[t, 0:1], lam_ref[t, 1:2]
        g1 = 2.0 * l0 * d_prod
        g2 = 2.0 * l1 * d_prod
        d_a = [
            d_prod,
            jnp.concatenate([g1 * a for a in a1], axis=0),
            jnp.concatenate([g2 * a for a in a2], axis=0),
        ]
        d_t = [d.T.astype(BF16) for d in d_a]
        d_a = [d.astype(BF16) for d in d_a]
        span = [(0, 1), (1, 4), (4, 9)]
        for e in range(0, edges, CH):
            up = lift[t, :, e : e + CH]
            d_up = jnp.zeros((width, CH), F32)
            for k, (lo, hi) in enumerate(span):
                d_base = dg(d_t[k], pool[lo * atoms : hi * atoms, e : e + CH], 1, 0)
                d_up = d_up + d_base * rad[t, k * width : (k + 1) * width, e : e + CH]
                der[k * width : (k + 1) * width, e : e + CH] = (d_base * up).astype(BF16)
            if t == 1:
                dlift[:, e : e + CH] = d_up.astype(BF16)
        return d_a

    def edge_rows(t, d_a):
        span = [(0, 1), (1, 4), (4, 9)]
        for e in range(0, edges, CH):
            pick = ohr[:, e : e + CH].astype(F32)
            for k, (lo, hi) in enumerate(span):
                q = dg(d_a[k], base[t, k * width : (k + 1) * width, e : e + CH], 1, 0)
                for m in range(lo, hi):
                    part = q[(m - lo) * atoms : (m - lo + 1) * atoms] * pick
                    line = jnp.sum(part, axis=0, keepdims=True)
                    if t == 1:
                        drow[m : m + 1, e : e + CH] = line
                    else:
                        drow[m : m + 1, e : e + CH] += line
        d_hidden = dg(jnp.concatenate(split(wout_ref[t]), axis=0), der[...], 1, 0)
        d_hidden = d_hidden[0:rh] + d_hidden[rh : 2 * rh]
        pre = pre_s[t]
        sig = jax.nn.sigmoid(pre)
        d_pre = d_hidden * (sig * (1.0 + pre * (1.0 - sig)))
        d_basis = dg3(win_ref[t], d_pre, 1, 0)
        gap = rows[3:4] - centres
        slope = jnp.sum(d_basis * basis_of() * gap, axis=0, keepdims=True) * (-2.0 * nb * nb)
        if t == 1:
            drow[9:10] = slope
        else:
            drow[9:10] += slope

    radial(0)
    prod1, a1_one, a2_one = pooled(0)
    h1 = h0 + dg3(prod1, wmix_ref[0], 1, 0)
    h_own[...] = h1.astype(BF16)
    second = exchange(1, lambda u: h_own, h_in, -1)
    h_in[here] = h_own[...]
    rone = jnp.broadcast_to(rone_ref[...], (8, width))
    energy1 = dg3(rone, h1, 1, 1)[0:1]
    radial(1)
    wt_h, wt_l = split(wup_ref[1].T)
    for c in second:
        c.wait_recv()

    feats = h_in[...].reshape(ghosts, width)
    ghost_lift = (dg(wt_h, feats, 1, 1) + dg(wt_l, feats, 1, 1)).astype(BF16)
    for e in range(0, edges, CH):
        lift[1, :, e : e + CH] = dg(ghost_lift, ohs[:, e : e + CH], 1, 0)
    prod2, a1_two, a2_two = pooled(1)
    h2 = h_own[...].astype(F32) + dg3(prod2, wmix_ref[1], 1, 0)
    ro_pre = dg3(rhid_ref[...], h2, 1, 1)
    eye = lax.broadcasted_iota(jnp.int32, (ro_pre.shape[0],) * 2, 0) == (
        lax.broadcasted_iota(jnp.int32, (ro_pre.shape[0],) * 2, 1)
    )
    rout = jnp.sum(jnp.where(eye, rout_ref[...], 0.0), axis=1, keepdims=True)
    ro_sig = jax.nn.sigmoid(ro_pre)
    energy2 = jnp.sum(ro_pre * ro_sig * rout, axis=0, keepdims=True)
    energy_ref[0, 0] = (energy1 + energy2) * atom_row

    d_ro = rout * atom_row * (ro_sig * (1.0 + ro_pre * (1.0 - ro_sig)))
    d_h2 = dg3(d_ro, rhid_ref[...], 0, 0)
    d_prod2 = dg3(d_h2, wmix_ref[1], 1, 1)
    d_a = pulled(1, d_prod2, a1_two, a2_two)
    third = []
    for t in range(tiles):
        d_ghost = dg(ohs[t * 128 : (t + 1) * 128], dlift[...], 1, 1)
        for j in range(4):
            if 4 * t + j < total:
                dl_out[4 * t + j] = d_ghost[32 * j : 32 * j + 32].astype(BF16)
        third += exchange(2, lambda u: dl_out.at[u], dl_in, 1, t)
    dl_in[here] = dl_out[here]
    edge_rows(1, d_a)
    for c in third:
        c.wait_recv()

    gathered = dl_in[0].astype(F32)
    for u in range(1, total):
        gathered = gathered + dl_in[u].astype(F32)
    d_h1 = d_h2 + dg3(gathered, wup_ref[1], 1, 1) + atom_col * rone_ref[...]
    d_prod1 = dg3(d_h1, wmix_ref[0], 1, 1)
    d_a = pulled(0, d_prod1, a1_one, a2_one)
    edge_rows(0, d_a)

    x, y, z, inner = rows[0:1], rows[1:2], rows[2:3], rows[4:5]
    env8 = inner * inner * (1.0 / mean_degree)
    d_env = drow[0:1] * rows[8:9]
    for m in range(1, 9):
        d_env = d_env + drow[m : m + 1] * rows[8 + m : 9 + m]
    d_dist = 2.0 * (drow[9:10] - 2.0 * d_env * inner)
    dh = [drow[m : m + 1] * env8 for m in range(9)]
    d_x = d_dist * x + s3 * dh[1] + s15 * (y * dh[4] + z * dh[6] + x * dh[7]) - s5 * x * dh[8]
    d_y = d_dist * y + s3 * dh[2] + s15 * (x * dh[4] + z * dh[5] - y * dh[7]) - s5 * y * dh[8]
    d_z = d_dist * z + s3 * dh[3] + s15 * (y * dh[5] + x * dh[6]) + 2.0 * s5 * z * dh[8]
    drow[0:1] = d_x / cutoff_radius
    drow[1:2] = d_y / cutoff_radius
    drow[2:3] = d_z / cutoff_radius
    drow[3:8] = jnp.zeros((5, edges), F32)
    d_rel = drow[0:8]
    d_hi = d_rel.astype(BF16).astype(F32)
    both = jnp.concatenate([d_hi, d_rel - d_hi], axis=0).astype(BF16)
    fourth = []
    for t in range(tiles):
        back = dg(both, ohs[t * 128 : (t + 1) * 128], 1, 1)
        dp_out[t] = back[0:8] + back[8:16]
        fourth += exchange(3, lambda u: dp_out.at[u // 4], dp_in, 1, t)
    dp_in[here] = dp_out[here // 4]
    own = dg(both, ohr[...], 1, 1)
    for c in fourth:
        c.wait_recv()
    fold = jnp.zeros((8, 128), F32)
    for u in range(total):
        j = u % 4
        inside = (lane >= 32 * j) & (lane < 32 * j + 32)
        fold = fold + jnp.where(inside, dp_in[u], 0.0)
    fold = fold + pltpu.roll(fold, 64, 1)
    fold = fold + pltpu.roll(fold, 32, 1)
    force = own[0:8] + own[8:16] - fold[:, 0:atoms]
    for a in range(3):
        force_ref[a, 0, 0] = force[a : a + 1]
    for c in sent:
        c.wait_send()


def local(
    sizes,
    positions,
    species,
    atom_count,
    edge_count,
    sender,
    receiver,
    image_shift,
    embed,
    radial_in,
    radial_out,
    w_up,
    lam,
    w_mix,
    read_one,
    read_hidden,
    read_out,
):
    atoms = positions.shape[-1]
    edges = sender.shape[-1]
    nspec, width = embed.shape
    rh = radial_in.shape[2]
    total = len(offsets_of(sizes))
    tiles = (total + 3) // 4
    ghosts = tiles * 128
    operands = (
        positions,
        species,
        atom_count,
        edge_count,
        sender,
        receiver,
        image_shift,
        embed,
        radial_in,
        radial_out,
        w_up,
        lam,
        w_mix,
        read_one.reshape(1, width),
        read_hidden.T,
        read_out.reshape(1, -1),
    )
    vmem = pl.BlockSpec(memory_space=pltpu.VMEM)
    energy, force = pl.pallas_call(
        functools.partial(kernel, sizes),
        out_shape=(
            jax.ShapeDtypeStruct((1, 1, 1, atoms), F32),
            jax.ShapeDtypeStruct((3, 1, 1, 1, atoms), F32),
        ),
        in_specs=[pl.BlockSpec(memory_space=pltpu.HBM)] * INPUTS,
        out_specs=(vmem, vmem),
        scratch_shapes=[pltpu.VMEM(a.shape, a.dtype) for a in operands]
        + [
            pltpu.VMEM((8, 128), F32),
            pltpu.VMEM((total, 8, 128), F32),
            pltpu.VMEM((atoms, width), BF16),
            pltpu.VMEM((4 * tiles, atoms, width), BF16),
            pltpu.VMEM((total, atoms, width), BF16),
            pltpu.VMEM((total, atoms, width), BF16),
            pltpu.VMEM((tiles, 8, 128), F32),
            pltpu.VMEM((total, 8, 128), F32),
            pltpu.VMEM(((nspec + 15) // 16 * 16, width), F32),
            pltpu.VMEM((ghosts, edges), BF16),
            pltpu.VMEM((atoms, edges), BF16),
            pltpu.VMEM((9 * atoms, edges), BF16),
            pltpu.VMEM((2, 3 * width, edges), F32),
            pltpu.VMEM((2, width, edges), F32),
            pltpu.VMEM((2, 3 * width, edges), BF16),
            pltpu.VMEM((2, rh, edges), F32),
            pltpu.VMEM((3 * width, edges), BF16),
            pltpu.VMEM((width, edges), BF16),
            pltpu.VMEM((24, edges), F32),
            pltpu.VMEM((16, edges), F32),
            pltpu.SemaphoreType.DMA((INPUTS,)),
            pltpu.SemaphoreType.DMA((4, total)),
            pltpu.SemaphoreType.DMA((4, total)),
        ],
        compiler_params=pltpu.CompilerParams(
            collective_id=0, has_side_effects=True, vmem_limit_bytes=64 * 1024 * 1024
        ),
    )(*operands)
    return energy, force


def solution(mesh):
    sizes = tuple(mesh.shape[a] for a in ("gx", "gy", "gz"))
    in_specs = (
        P(None, "gx", "gy", "gz", None),
        P("gx", "gy", "gz", None),
        P("gx", "gy", "gz"),
        P("gx", "gy", "gz"),
        P("gx", "gy", "gz", None),
        P("gx", "gy", "gz", None),
        P(None, "gx", "gy", "gz", None),
        P(),
        P(),
        P(),
        P(),
        P(),
        P(),
        P(),
        P(),
        P(),
    )
    out_specs = (P("gx", "gy", "gz", None), P(None, "gx", "gy", "gz", None))
    return jax.shard_map(
        functools.partial(local, sizes),
        mesh=mesh,
        in_specs=in_specs,
        out_specs=out_specs,
        check_vma=False,
    )
```

```python
import functools
import itertools

import jax
import jax.numpy as jnp
from jax import lax
from jax.experimental import pallas as pl
from jax.experimental.pallas import tpu as pltpu
from jax.sharding import PartitionSpec as P

cutoff_radius = 5.0
lattice_step = 2.25
mean_degree = 8.0
F32 = jnp.float32
BF16 = jnp.bfloat16
MESH = pl.DeviceIdType.MESH
CH = 256
INPUTS = 16


def dg(a, b, ca, cb):
    return lax.dot_general(a, b, (((ca,), (cb,)), ((), ())), preferred_element_type=F32)


def split(x):
    hi = x.astype(BF16)
    return hi, (x - hi.astype(F32)).astype(BF16)


def dg3(a, b, ca, cb):
    ah, al = split(a)
    bh, bl = split(b)
    left = jnp.concatenate([ah, ah, al], axis=ca)
    right = jnp.concatenate([bh, bl, bh], axis=cb)
    return dg(left, right, ca, cb)


def parts(x):
    p1 = x.astype(BF16).astype(F32)
    p2 = (x - p1).astype(BF16).astype(F32)
    p3 = x - p1 - p2
    return jnp.concatenate([p1, p2, p3, jnp.zeros_like(x)], axis=0).astype(BF16)


def whole(y):
    return y[0:8] + y[8:16] + y[16:24]


def offsets_of(sizes):
    per_axis = [(-1, 0, 1) if n >= 3 else (-1, 0) if n == 2 else (0,) for n in sizes]
    return list(itertools.product(*per_axis))


def kernel(
    sizes,
    *refs,
):
    hbm = refs[:INPUTS]
    held = refs[INPUTS + 1 : 2 * INPUTS + 1]
    body(sizes, hbm, refs[INPUTS], held, *refs[2 * INPUTS + 1 :])


def body(
    sizes,
    hbm,
    out_ref,
    held,
    own8,
    gpos_in,
    h_own,
    h_in,
    dl_out,
    dl_in,
    dp_out,
    dp_in,
    emb_s,
    ohs,
    ohr,
    pool,
    rad,
    lift,
    base,
    pre_s,
    der,
    dlift,
    rows,
    drow,
    in_sem,
    send_sem,
    recv_sem,
):
    (
        pos_ref,
        spec_ref,
        acount_ref,
        ecount_ref,
        sender_ref,
        receiver_ref,
        shift_ref,
        embed_ref,
        win_ref,
        wout_ref,
        wup_ref,
        lam_ref,
        wmix_ref,
        rone_ref,
        rhid_ref,
        rout_ref,
    ) = held
    fetch = [
        pltpu.make_async_copy(src, dst, in_sem.at[i])
        for i, (src, dst) in enumerate(zip(hbm, held))
    ]
    for c in fetch:
        c.start()
    atoms = pos_ref.shape[-1]
    edges = sender_ref.shape[-1]
    nb = win_ref.shape[1]
    rh = win_ref.shape[2]
    width = embed_ref.shape[1]
    nspec = embed_ref.shape[0]
    spad = emb_s.shape[0]
    offs = offsets_of(sizes)
    total = len(offs)
    tiles = dp_out.shape[0]
    ghosts = tiles * 128
    here = offs.index(tuple(0 for _ in sizes))
    me = [lax.axis_index(a) for a in ("gx", "gy", "gz")]

    def device(off, sign):
        return tuple(
            lax.rem(m + (sign * o) % n, n) if o else m for m, o, n in zip(me, off, sizes)
        )

    others = [u for u in range(total) if u != here]

    barrier = pltpu.get_barrier_semaphore()
    for u in others:
        pl.semaphore_signal(barrier, inc=1, device_id=device(offs[u], 1), device_id_type=MESH)

    own8[...] = jnp.zeros_like(own8)
    fetch[0].wait()
    fetch[1].wait()
    mine = jnp.concatenate(
        [pos_ref[a, 0, 0] for a in range(3)] + [spec_ref[0, 0].astype(F32)], axis=0
    )
    own8[0:4, :] = jnp.concatenate([mine] * 4, axis=1)
    pl.semaphore_wait(barrier, len(others))

    def copy(phase, u, src, dst, sign):
        return pltpu.make_async_remote_copy(
            src_ref=src,
            dst_ref=dst,
            send_sem=send_sem.at[phase, u],
            recv_sem=recv_sem.at[phase, u],
            device_id=device(offs[u], sign),
            device_id_type=MESH,
        )

    sent = []

    def exchange(phase, source, target, sign, tile=None):
        started = [
            copy(phase, u, source(u), target.at[u], sign)
            for u in others
            if tile is None or u // 4 == tile
        ]
        for c in started:
            c.start()
        sent.extend(started)
        return started

    first = exchange(0, lambda u: own8, gpos_in, -1)

    gpos_in[here] = own8[...]
    for c in fetch[2:]:
        c.wait()
    send_id = sender_ref[0, 0]
    block = jnp.right_shift(send_id, 5)
    slot = send_id - block * 32
    bx = (block >= 9).astype(jnp.int32) + (block >= 18).astype(jnp.int32)
    rest = block - 9 * bx
    by = (rest >= 3).astype(jnp.int32) + (rest >= 6).astype(jnp.int32)
    bz = rest - 3 * by
    flat = jnp.zeros_like(block)
    for d, n in zip((bx, by, bz), sizes):
        if n >= 3:
            flat = flat * 3 + d
        elif n == 2:
            flat = flat * 2 + jnp.where(d == 1, 1, 0)
    ghost_id = flat * 32 + slot
    sub = lax.broadcasted_iota(jnp.int32, (128, CH), 0)
    for e in range(0, edges, CH):
        for t in range(tiles):
            ohs[t * 128 : (t + 1) * 128, e : e + CH] = jnp.where(
                sub == ghost_id[:, e : e + CH] - t * 128, 1.0, 0.0
            ).astype(BF16)
    recv_id = receiver_ref[0, 0]
    near = lax.broadcasted_iota(jnp.int32, (atoms, edges), 0) == recv_id
    ohr[...] = jnp.where(near, 1.0, 0.0).astype(BF16)
    at_recv = whole(dg(parts(own8[...])[:, 0:atoms], ohr[...], 1, 0))
    emb_s[...] = jnp.zeros_like(emb_s)
    emb_s[0:nspec, :] = embed_ref[...]
    emb = emb_s[...].astype(BF16)
    wu_h, wu_l = split(wup_ref[0])
    table = (dg(emb, wu_h, 1, 0) + dg(emb, wu_l, 1, 0)).astype(BF16)
    kind = lax.broadcasted_iota(jnp.int32, (spad, 128), 0).astype(F32)
    own_kind = jnp.where(kind == own8[3:4, :], 1.0, 0.0).astype(BF16)
    h0 = dg(own_kind, emb, 0, 0)[0:atoms]
    valid = lax.broadcasted_iota(jnp.int32, (1, edges), 1) < ecount_ref[0]
    atom_row = (lax.broadcasted_iota(jnp.int32, (1, atoms), 1) < acount_ref[0]).astype(F32)
    atom_col = (lax.broadcasted_iota(jnp.int32, (atoms, width), 0) < acount_ref[0]).astype(F32)
    if h_in.shape[0] > total:
        h_in[total:] = jnp.zeros((h_in.shape[0] - total, atoms, width), BF16)

    for c in first:
        c.wait_recv()

    lane = lax.broadcasted_iota(jnp.int32, (8, 128), 1)
    cols = []
    for t in range(tiles):
        tile = jnp.zeros((8, 128), F32)
        for j in range(4):
            if 4 * t + j < total:
                inside = (lane >= 32 * j) & (lane < 32 * j + 32)
                tile = jnp.where(inside, gpos_in[4 * t + j], tile)
        cols.append(tile)
    gpos = jnp.concatenate(cols, axis=1)
    gkind = jnp.concatenate(
        [jnp.where(kind == c[3:4, :], 1.0, 0.0).astype(BF16) for c in cols], axis=1
    )
    ghost_lift = dg(table, gkind, 0, 0).astype(BF16)
    lhs = jnp.concatenate([ghost_lift, parts(gpos)], axis=0)
    at_send = []
    for e in range(0, edges, CH):
        got = dg(lhs, ohs[:, e : e + CH], 1, 0)
        lift[0, :, e : e + CH] = got[0:width]
        at_send.append(whole(got[width:]))
    at_send = jnp.concatenate(at_send, axis=1)

    def axis(a, n, cells):
        length = n * cells * lattice_step
        moved = at_send[a : a + 1] + shift_ref[a, 0, 0].astype(F32) * length
        return (moved - at_recv[a : a + 1]) / cutoff_radius

    x = axis(0, sizes[0], 4)
    y = axis(1, sizes[1], 4)
    z = axis(2, sizes[2], atoms // 16)
    dist2 = x * x + y * y + z * z
    inner = jnp.where(valid, jnp.maximum(1.0 - dist2, 0.0), 0.0)
    env = inner * inner
    s3, s5, s15 = 3.0**0.5, 5.0**0.5, 15.0**0.5
    harm = [
        jnp.ones_like(x),
        s3 * x,
        s3 * y,
        s3 * z,
        s15 * x * y,
        s15 * y * z,
        s15 * x * z,
        0.5 * s15 * (x * x - y * y),
        0.5 * s5 * (2.0 * z * z - x * x - y * y),
    ]
    rows[0:1] = x
    rows[1:2] = y
    rows[2:3] = z
    rows[3:4] = dist2
    rows[4:5] = inner
    for m in range(9):
        rows[8 + m : 9 + m] = harm[m] * (1.0 / mean_degree)
        weight = harm[m] * env * (1.0 / mean_degree)
        pool[atoms * m : atoms * (m + 1), :] = jnp.where(near, weight, 0.0).astype(BF16)

    centres = lax.broadcasted_iota(jnp.int32, (nb, CH), 0).astype(F32) / (nb - 1)

    def gap_of(e):
        return rows[3:4, e : e + CH] - centres

    def radial(t):
        wi = win_ref[t]
        wh = wi.astype(BF16).astype(F32)
        wl = wi - wh
        wi = jnp.concatenate([wh, wh, wl, wl], axis=0).T.astype(BF16)
        wo = wout_ref[t]
        oh = wo.astype(BF16).astype(F32)
        left = jnp.concatenate([oh, oh, wo - oh], axis=0).T.astype(BF16)
        for e in range(0, edges, CH):
            basis = jnp.exp(-jnp.square(gap_of(e) * nb))
            bh = basis.astype(BF16).astype(F32)
            bl = basis - bh
            pre = dg(wi, jnp.concatenate([bh, bl, bh, bl], axis=0).astype(BF16), 1, 0)
            pre_s[t, :, e : e + CH] = pre
            hh, hl = split(pre * jax.nn.sigmoid(pre))
            rad[t, :, e : e + CH] = dg(left, jnp.concatenate([hh, hl, hh], axis=0), 1, 0)

    def pooled(t):
        for e in range(0, edges, CH):
            up = lift[t, :, e : e + CH]
            for k in range(3):
                base[t, k * width : (k + 1) * width, e : e + CH] = (
                    rad[t, k * width : (k + 1) * width, e : e + CH] * up
                ).astype(BF16)
        a0 = dg(pool[0:atoms], base[t, 0:width], 1, 1)
        a1 = dg(pool[atoms : 4 * atoms], base[t, width : 2 * width], 1, 1)
        a2 = dg(pool[4 * atoms : 9 * atoms], base[t, 2 * width : 3 * width], 1, 1)
        a1 = [a1[atoms * m : atoms * (m + 1)] for m in range(3)]
        a2 = [a2[atoms * m : atoms * (m + 1)] for m in range(5)]
        l0, l1 = lam_ref[t, 0:1], lam_ref[t, 1:2]
        q1 = sum(a * a for a in a1)
        q2 = sum(a * a for a in a2)
        return a0 + l0 * q1 + l1 * q2, a1, a2

    def pulled(t, d_prod, a1, a2):
        l0, l1 = lam_ref[t, 0:1], lam_ref[t, 1:2]
        g1 = 2.0 * l0 * d_prod
        g2 = 2.0 * l1 * d_prod
        d_a = [
            d_prod,
            jnp.concatenate([g1 * a for a in a1], axis=0),
            jnp.concatenate([g2 * a for a in a2], axis=0),
        ]
        d_t = [d.T.astype(BF16) for d in d_a]
        d_a = [d.astype(BF16) for d in d_a]
        span = [(0, 1), (1, 4), (4, 9)]
        for e in range(0, edges, CH):
            up = lift[t, :, e : e + CH]
            d_up = jnp.zeros((width, CH), F32)
            for k, (lo, hi) in enumerate(span):
                d_base = dg(d_t[k], pool[lo * atoms : hi * atoms, e : e + CH], 1, 0)
                d_up = d_up + d_base * rad[t, k * width : (k + 1) * width, e : e + CH]
                der[k * width : (k + 1) * width, e : e + CH] = (d_base * up).astype(BF16)
            if t == 1:
                dlift[:, e : e + CH] = d_up.astype(BF16)
        return d_a

    def edge_rows(t, d_a):
        span = [(0, 1), (1, 4), (4, 9)]
        wo = jnp.concatenate(split(wout_ref[t]), axis=0)
        wi = win_ref[t]
        wh = wi.astype(BF16).astype(F32)
        wi = jnp.concatenate([wh, wh, wi - wh], axis=1).astype(BF16)
        for e in range(0, edges, CH):
            pick = ohr[:, e : e + CH].astype(F32)
            for k, (lo, hi) in enumerate(span):
                q = dg(d_a[k], base[t, k * width : (k + 1) * width, e : e + CH], 1, 0)
                for m in range(lo, hi):
                    part = q[(m - lo) * atoms : (m - lo + 1) * atoms] * pick
                    line = jnp.sum(part, axis=0, keepdims=True)
                    if t == 1:
                        drow[m : m + 1, e : e + CH] = line
                    else:
                        drow[m : m + 1, e : e + CH] += line
            d_hidden = dg(wo, der[:, e : e + CH], 1, 0)
            d_hidden = d_hidden[0:rh] + d_hidden[rh : 2 * rh]
            pre = pre_s[t, :, e : e + CH]
            sig = jax.nn.sigmoid(pre)
            ph, pl_ = split(d_hidden * (sig * (1.0 + pre * (1.0 - sig))))
            d_basis = dg(wi, jnp.concatenate([ph, pl_, ph], axis=0), 1, 0)
            gap = gap_of(e)
            d_basis = d_basis * jnp.exp(-jnp.square(gap * nb)) * gap
            slope = jnp.sum(d_basis, axis=0, keepdims=True) * (-2.0 * nb * nb)
            if t == 1:
                drow[9:10, e : e + CH] = slope
            else:
                drow[9:10, e : e + CH] += slope

    radial(0)
    prod1, a1_one, a2_one = pooled(0)
    h1 = h0 + dg3(prod1, wmix_ref[0], 1, 0)
    h_own[...] = h1.astype(BF16)
    second = exchange(1, lambda u: h_own, h_in, -1)
    h_in[here] = h_own[...]
    rone = jnp.broadcast_to(rone_ref[...], (8, width))
    energy1 = dg3(rone, h1, 1, 1)[0:1]
    radial(1)
    wt_h, wt_l = split(wup_ref[1].T)
    for c in second:
        c.wait_recv()

    feats = h_in[...].reshape(ghosts, width)
    ghost_lift = (dg(wt_h, feats, 1, 1) + dg(wt_l, feats, 1, 1)).astype(BF16)
    for e in range(0, edges, CH):
        lift[1, :, e : e + CH] = dg(ghost_lift, ohs[:, e : e + CH], 1, 0)
    prod2, a1_two, a2_two = pooled(1)
    h2 = h_own[...].astype(F32) + dg3(prod2, wmix_ref[1], 1, 0)
    ro_pre = dg3(rhid_ref[...], h2, 1, 1)
    eye = lax.broadcasted_iota(jnp.int32, (ro_pre.shape[0],) * 2, 0) == (
        lax.broadcasted_iota(jnp.int32, (ro_pre.shape[0],) * 2, 1)
    )
    rout = jnp.sum(jnp.where(eye, rout_ref[...], 0.0), axis=1, keepdims=True)
    ro_sig = jax.nn.sigmoid(ro_pre)
    energy2 = jnp.sum(ro_pre * ro_sig * rout, axis=0, keepdims=True)
    out_ref[...] = jnp.zeros_like(out_ref)
    out_ref[3:4, 0:atoms] = (energy1 + energy2) * atom_row

    d_ro = rout * atom_row * (ro_sig * (1.0 + ro_pre * (1.0 - ro_sig)))
    d_h2 = dg3(d_ro, rhid_ref[...], 0, 0)
    d_prod2 = dg3(d_h2, wmix_ref[1], 1, 1)
    d_a = pulled(1, d_prod2, a1_two, a2_two)
    third = []
    for t in range(tiles):
        d_ghost = dg(ohs[t * 128 : (t + 1) * 128], dlift[...], 1, 1)
        for j in range(4):
            if 4 * t + j < total:
                dl_out[4 * t + j] = d_ghost[32 * j : 32 * j + 32].astype(BF16)
        third += exchange(2, lambda u: dl_out.at[u], dl_in, 1, t)
    dl_in[here] = dl_out[here]
    edge_rows(1, d_a)
    for c in third:
        c.wait_recv()

    gathered = dl_in[0].astype(F32)
    for u in range(1, total):
        gathered = gathered + dl_in[u].astype(F32)
    d_h1 = d_h2 + dg3(gathered, wup_ref[1], 1, 1) + atom_col * rone_ref[...]
    d_prod1 = dg3(d_h1, wmix_ref[0], 1, 1)
    d_a = pulled(0, d_prod1, a1_one, a2_one)
    edge_rows(0, d_a)

    x, y, z, inner = rows[0:1], rows[1:2], rows[2:3], rows[4:5]
    env8 = inner * inner * (1.0 / mean_degree)
    d_env = drow[0:1] * rows[8:9]
    for m in range(1, 9):
        d_env = d_env + drow[m : m + 1] * rows[8 + m : 9 + m]
    d_dist = 2.0 * (drow[9:10] - 2.0 * d_env * inner)
    dh = [drow[m : m + 1] * env8 for m in range(9)]
    d_x = d_dist * x + s3 * dh[1] + s15 * (y * dh[4] + z * dh[6] + x * dh[7]) - s5 * x * dh[8]
    d_y = d_dist * y + s3 * dh[2] + s15 * (x * dh[4] + z * dh[5] - y * dh[7]) - s5 * y * dh[8]
    d_z = d_dist * z + s3 * dh[3] + s15 * (y * dh[5] + x * dh[6]) + 2.0 * s5 * z * dh[8]
    drow[0:1] = d_x / cutoff_radius
    drow[1:2] = d_y / cutoff_radius
    drow[2:3] = d_z / cutoff_radius
    drow[3:8] = jnp.zeros((5, edges), F32)
    d_rel = drow[0:8]
    d_hi = d_rel.astype(BF16).astype(F32)
    both = jnp.concatenate([d_hi, d_rel - d_hi], axis=0).astype(BF16)
    fourth = []
    for t in range(tiles):
        back = dg(ohs[t * 128 : (t + 1) * 128], both, 1, 1).T
        dp_out[t] = back[0:8] + back[8:16]
        fourth += exchange(3, lambda u: dp_out.at[u // 4], dp_in, 1, t)
    dp_in[here] = dp_out[here // 4]
    own = dg(both, ohr[...], 1, 1)
    for c in fourth:
        c.wait_recv()
    fold = jnp.zeros((8, 128), F32)
    for u in range(total):
        j = u % 4
        inside = (lane >= 32 * j) & (lane < 32 * j + 32)
        fold = fold + jnp.where(inside, dp_in[u], 0.0)
    fold = fold + pltpu.roll(fold, 64, 1)
    fold = fold + pltpu.roll(fold, 32, 1)
    force = own[0:8] + own[8:16] - fold[:, 0:atoms]
    out_ref[0:3, 0:atoms] = force[0:3]
    for c in sent:
        c.wait_send()


def local(
    sizes,
    positions,
    species,
    atom_count,
    edge_count,
    sender,
    receiver,
    image_shift,
    embed,
    radial_in,
    radial_out,
    w_up,
    lam,
    w_mix,
    read_one,
    read_hidden,
    read_out,
):
    atoms = positions.shape[-1]
    edges = sender.shape[-1]
    nspec, width = embed.shape
    rh = radial_in.shape[2]
    total = len(offsets_of(sizes))
    tiles = (total + 3) // 4
    ghosts = tiles * 128
    operands = (
        positions,
        species,
        atom_count,
        edge_count,
        sender,
        receiver,
        image_shift,
        embed,
        radial_in,
        radial_out,
        w_up,
        lam,
        w_mix,
        read_one.reshape(1, width),
        read_hidden.T,
        read_out.reshape(1, -1),
    )
    vmem = pl.BlockSpec(memory_space=pltpu.VMEM)
    out = pl.pallas_call(
        functools.partial(kernel, sizes),
        out_shape=jax.ShapeDtypeStruct((8, 128), F32),
        in_specs=[pl.BlockSpec(memory_space=pltpu.HBM)] * INPUTS,
        out_specs=vmem,
        scratch_shapes=[pltpu.VMEM(a.shape, a.dtype) for a in operands]
        + [
            pltpu.VMEM((8, 128), F32),
            pltpu.VMEM((total, 8, 128), F32),
            pltpu.VMEM((atoms, width), BF16),
            pltpu.VMEM((4 * tiles, atoms, width), BF16),
            pltpu.VMEM((total, atoms, width), BF16),
            pltpu.VMEM((total, atoms, width), BF16),
            pltpu.VMEM((tiles, 8, 128), F32),
            pltpu.VMEM((total, 8, 128), F32),
            pltpu.VMEM(((nspec + 15) // 16 * 16, width), F32),
            pltpu.VMEM((ghosts, edges), BF16),
            pltpu.VMEM((atoms, edges), BF16),
            pltpu.VMEM((9 * atoms, edges), BF16),
            pltpu.VMEM((2, 3 * width, edges), F32),
            pltpu.VMEM((2, width, edges), F32),
            pltpu.VMEM((2, 3 * width, edges), BF16),
            pltpu.VMEM((2, rh, edges), F32),
            pltpu.VMEM((3 * width, edges), BF16),
            pltpu.VMEM((width, edges), BF16),
            pltpu.VMEM((24, edges), F32),
            pltpu.VMEM((16, edges), F32),
            pltpu.SemaphoreType.DMA((INPUTS,)),
            pltpu.SemaphoreType.DMA((4, total)),
            pltpu.SemaphoreType.DMA((4, total)),
        ],
        compiler_params=pltpu.CompilerParams(
            collective_id=0, has_side_effects=True, vmem_limit_bytes=64 * 1024 * 1024
        ),
    )(*operands)
    energy = out[3, 0:atoms].reshape(1, 1, 1, atoms)
    return energy, out[0:3, 0:atoms].reshape(3, 1, 1, 1, atoms)


def solution(mesh):
    sizes = tuple(mesh.shape[a] for a in ("gx", "gy", "gz"))
    in_specs = (
        P(None, "gx", "gy", "gz", None),
        P("gx", "gy", "gz", None),
        P("gx", "gy", "gz"),
        P("gx", "gy", "gz"),
        P("gx", "gy", "gz", None),
        P("gx", "gy", "gz", None),
        P(None, "gx", "gy", "gz", None),
        P(),
        P(),
        P(),
        P(),
        P(),
        P(),
        P(),
        P(),
        P(),
    )
    out_specs = (P("gx", "gy", "gz", None), P(None, "gx", "gy", "gz", None))
    return jax.shard_map(
        functools.partial(local, sizes),
        mesh=mesh,
        in_specs=in_specs,
        out_specs=out_specs,
        check_vma=False,
    )
```

```python
import functools
import itertools

import jax
import jax.numpy as jnp
from jax import lax
from jax.experimental import pallas as pl
from jax.experimental.pallas import tpu as pltpu
from jax.sharding import PartitionSpec as P

cutoff_radius = 5.0
lattice_step = 2.25
mean_degree = 8.0
F32 = jnp.float32
BF16 = jnp.bfloat16
MESH = pl.DeviceIdType.MESH
CH = 256
INPUTS = 16


def dg(a, b, ca, cb):
    return lax.dot_general(a, b, (((ca,), (cb,)), ((), ())), preferred_element_type=F32)


def split(x):
    hi = x.astype(BF16)
    return hi, (x - hi.astype(F32)).astype(BF16)


def dg3(a, b, ca, cb):
    ah, al = split(a)
    bh, bl = split(b)
    return dg(ah, bh, ca, cb) + (dg(ah, bl, ca, cb) + dg(al, bh, ca, cb))


def parts(x):
    p1 = x.astype(BF16).astype(F32)
    p2 = (x - p1).astype(BF16).astype(F32)
    p3 = x - p1 - p2
    return jnp.concatenate([p1, p2, p3, jnp.zeros_like(x)], axis=0).astype(BF16)


def whole(y):
    return y[0:8] + y[8:16] + y[16:24]


def offsets_of(sizes):
    per_axis = [(-1, 0, 1) if n >= 3 else (-1, 0) if n == 2 else (0,) for n in sizes]
    return list(itertools.product(*per_axis))


def kernel(
    sizes,
    *refs,
):
    hbm = refs[:INPUTS]
    energy_ref, force_ref = refs[INPUTS : INPUTS + 2]
    held = refs[INPUTS + 2 : 2 * INPUTS + 2]
    body(sizes, hbm, energy_ref, force_ref, held, *refs[2 * INPUTS + 2 :])


def body(
    sizes,
    hbm,
    energy_ref,
    force_ref,
    held,
    own8,
    gpos_in,
    h_own,
    h_in,
    dl_out,
    dl_in,
    dp_out,
    dp_in,
    emb_s,
    ohs,
    ohr,
    pool,
    rad,
    lift,
    base,
    pre_s,
    der,
    dlift,
    rows,
    drow,
    in_sem,
    send_sem,
    recv_sem,
):
    (
        pos_ref,
        spec_ref,
        acount_ref,
        ecount_ref,
        sender_ref,
        receiver_ref,
        shift_ref,
        embed_ref,
        win_ref,
        wout_ref,
        wup_ref,
        lam_ref,
        wmix_ref,
        rone_ref,
        rhid_ref,
        rout_ref,
    ) = held
    fetch = [
        pltpu.make_async_copy(src, dst, in_sem.at[i])
        for i, (src, dst) in enumerate(zip(hbm, held))
    ]
    atoms = pos_ref.shape[-1]
    edges = sender_ref.shape[-1]
    nb = win_ref.shape[1]
    rh = win_ref.shape[2]
    width = embed_ref.shape[1]
    nspec = embed_ref.shape[0]
    spad = emb_s.shape[0]
    offs = offsets_of(sizes)
    total = len(offs)
    tiles = dp_out.shape[0]
    ghosts = tiles * 128
    here = offs.index(tuple(0 for _ in sizes))
    me = [lax.axis_index(a) for a in ("gx", "gy", "gz")]

    def device(off, sign):
        return tuple(
            lax.rem(m + (sign * o) % n, n) if o else m for m, o, n in zip(me, off, sizes)
        )

    others = [u for u in range(total) if u != here]

    barrier = pltpu.get_barrier_semaphore()
    for u in others:
        pl.semaphore_signal(barrier, inc=1, device_id=device(offs[u], 1), device_id_type=MESH)
    for c in fetch:
        c.start()

    own8[...] = jnp.zeros_like(own8)
    fetch[0].wait()
    fetch[1].wait()
    mine = jnp.concatenate(
        [pos_ref[a, 0, 0] for a in range(3)] + [spec_ref[0, 0].astype(F32)], axis=0
    )
    own8[0:4, :] = jnp.concatenate([mine] * 4, axis=1)
    pl.semaphore_wait(barrier, len(others))

    def copy(phase, u, src, dst, sign):
        return pltpu.make_async_remote_copy(
            src_ref=src,
            dst_ref=dst,
            send_sem=send_sem.at[phase, u],
            recv_sem=recv_sem.at[phase, u],
            device_id=device(offs[u], sign),
            device_id_type=MESH,
        )

    def exchange(phase, source, target, sign, tile=None):
        started = [
            copy(phase, u, source(u), target.at[u], sign)
            for u in others
            if tile is None or u // 4 == tile
        ]
        for c in started:
            c.start()
        return started

    first = exchange(0, lambda u: own8, gpos_in, -1)

    gpos_in[here] = own8[...]
    for c in fetch[2:]:
        c.wait()
    send_id = sender_ref[0, 0]
    block = jnp.right_shift(send_id, 5)
    slot = send_id - block * 32
    bx = (block >= 9).astype(jnp.int32) + (block >= 18).astype(jnp.int32)
    rest = block - 9 * bx
    by = (rest >= 3).astype(jnp.int32) + (rest >= 6).astype(jnp.int32)
    bz = rest - 3 * by
    flat = jnp.zeros_like(block)
    for d, n in zip((bx, by, bz), sizes):
        if n >= 3:
            flat = flat * 3 + d
        elif n == 2:
            flat = flat * 2 + jnp.where(d == 1, 1, 0)
    ghost_id = flat * 32 + slot
    sub = lax.broadcasted_iota(jnp.int32, (128, CH), 0)
    for e in range(0, edges, CH):
        for t in range(tiles):
            ohs[t * 128 : (t + 1) * 128, e : e + CH] = jnp.where(
                sub == ghost_id[:, e : e + CH] - t * 128, 1.0, 0.0
            ).astype(BF16)
    recv_id = receiver_ref[0, 0]
    near = lax.broadcasted_iota(jnp.int32, (atoms, edges), 0) == recv_id
    ohr[...] = jnp.where(near, 1.0, 0.0).astype(BF16)
    at_recv = whole(dg(parts(own8[...])[:, 0:atoms], ohr[...], 1, 0))
    emb_s[...] = jnp.zeros_like(emb_s)
    emb_s[0:nspec, :] = embed_ref[...]
    emb = emb_s[...].astype(BF16)
    wu_h, wu_l = split(wup_ref[0])
    table = (dg(emb, wu_h, 1, 0) + dg(emb, wu_l, 1, 0)).astype(BF16)
    kind = lax.broadcasted_iota(jnp.int32, (spad, 128), 0).astype(F32)
    own_kind = jnp.where(kind == own8[3:4, :], 1.0, 0.0).astype(BF16)
    h0 = dg(own_kind, emb, 0, 0)[0:atoms]
    valid = lax.broadcasted_iota(jnp.int32, (1, edges), 1) < ecount_ref[0]
    atom_row = (lax.broadcasted_iota(jnp.int32, (1, atoms), 1) < acount_ref[0]).astype(F32)
    atom_col = (lax.broadcasted_iota(jnp.int32, (atoms, width), 0) < acount_ref[0]).astype(F32)
    if h_in.shape[0] > total:
        h_in[total:] = jnp.zeros((h_in.shape[0] - total, atoms, width), BF16)

    for c in first:
        c.wait_recv()

    lane = lax.broadcasted_iota(jnp.int32, (8, 128), 1)
    cols = []
    for t in range(tiles):
        tile = jnp.zeros((8, 128), F32)
        for j in range(4):
            if 4 * t + j < total:
                inside = (lane >= 32 * j) & (lane < 32 * j + 32)
                tile = jnp.where(inside, gpos_in[4 * t + j], tile)
        cols.append(tile)
    gpos = jnp.concatenate(cols, axis=1)
    gkind = jnp.concatenate(
        [jnp.where(kind == c[3:4, :], 1.0, 0.0).astype(BF16) for c in cols], axis=1
    )
    ghost_lift = dg(table, gkind, 0, 0).astype(BF16)
    lhs = jnp.concatenate([ghost_lift, parts(gpos)], axis=0)
    at_send = []
    for e in range(0, edges, CH):
        got = dg(lhs, ohs[:, e : e + CH], 1, 0)
        lift[0, :, e : e + CH] = got[0:width]
        at_send.append(whole(got[width:]))
    at_send = jnp.concatenate(at_send, axis=1)

    def axis(a, n, cells):
        length = n * cells * lattice_step
        moved = at_send[a : a + 1] + shift_ref[a, 0, 0].astype(F32) * length
        return (moved - at_recv[a : a + 1]) / cutoff_radius

    x = axis(0, sizes[0], 4)
    y = axis(1, sizes[1], 4)
    z = axis(2, sizes[2], atoms // 16)
    dist2 = x * x + y * y + z * z
    inner = jnp.where(valid, jnp.maximum(1.0 - dist2, 0.0), 0.0)
    env = inner * inner
    s3, s5, s15 = 3.0**0.5, 5.0**0.5, 15.0**0.5
    harm = [
        jnp.ones_like(x),
        s3 * x,
        s3 * y,
        s3 * z,
        s15 * x * y,
        s15 * y * z,
        s15 * x * z,
        0.5 * s15 * (x * x - y * y),
        0.5 * s5 * (2.0 * z * z - x * x - y * y),
    ]
    rows[0:1] = x
    rows[1:2] = y
    rows[2:3] = z
    rows[3:4] = dist2
    rows[4:5] = inner
    for m in range(9):
        rows[8 + m : 9 + m] = harm[m] * (1.0 / mean_degree)
        weight = harm[m] * env * (1.0 / mean_degree)
        pool[atoms * m : atoms * (m + 1), :] = jnp.where(near, weight, 0.0).astype(BF16)

    centres = lax.broadcasted_iota(jnp.int32, (nb, edges), 0).astype(F32) / (nb - 1)

    def basis_of():
        return jnp.exp(-jnp.square((rows[3:4] - centres) * nb))

    def radial(t):
        basis = basis_of()
        bh = basis.astype(BF16).astype(F32)
        bl = basis - bh
        wi = win_ref[t]
        wh = wi.astype(BF16).astype(F32)
        wl = wi - wh
        pre = dg(
            jnp.concatenate([wh, wh, wl, wl], axis=0).astype(BF16),
            jnp.concatenate([bh, bl, bh, bl], axis=0).astype(BF16),
            0,
            0,
        )
        pre_s[t] = pre
        hidden = pre * jax.nn.sigmoid(pre)
        hh, hl = split(hidden)
        wo = wout_ref[t]
        oh = wo.astype(BF16).astype(F32)
        left = jnp.concatenate([oh, oh, wo - oh], axis=0).T.astype(BF16)
        right = jnp.concatenate([hh, hl, hh], axis=0)
        for e in range(0, edges, CH):
            rad[t, :, e : e + CH] = dg(left, right[:, e : e + CH], 1, 0)

    def pooled(t):
        for e in range(0, edges, CH):
            up = lift[t, :, e : e + CH]
            for k in range(3):
                base[t, k * width : (k + 1) * width, e : e + CH] = (
                    rad[t, k * width : (k + 1) * width, e : e + CH] * up
                ).astype(BF16)
        a0 = dg(pool[0:atoms], base[t, 0:width], 1, 1)
        a1 = dg(pool[atoms : 4 * atoms], base[t, width : 2 * width], 1, 1)
        a2 = dg(pool[4 * atoms : 9 * atoms], base[t, 2 * width : 3 * width], 1, 1)
        a1 = [a1[atoms * m : atoms * (m + 1)] for m in range(3)]
        a2 = [a2[atoms * m : atoms * (m + 1)] for m in range(5)]
        l0, l1 = lam_ref[t, 0:1], lam_ref[t, 1:2]
        q1 = sum(a * a for a in a1)
        q2 = sum(a * a for a in a2)
        return a0 + l0 * q1 + l1 * q2, a1, a2

    def pulled(t, d_prod, a1, a2):
        l0, l1 = lam_ref[t, 0:1], lam_ref[t, 1:2]
        g1 = 2.0 * l0 * d_prod
        g2 = 2.0 * l1 * d_prod
        d_a = [
            d_prod,
            jnp.concatenate([g1 * a for a in a1], axis=0),
            jnp.concatenate([g2 * a for a in a2], axis=0),
        ]
        d_t = [d.T.astype(BF16) for d in d_a]
        d_a = [d.astype(BF16) for d in d_a]
        span = [(0, 1), (1, 4), (4, 9)]
        for e in range(0, edges, CH):
            up = lift[t, :, e : e + CH]
            d_up = jnp.zeros((width, CH), F32)
            for k, (lo, hi) in enumerate(span):
                d_base = dg(d_t[k], pool[lo * atoms : hi * atoms, e : e + CH], 1, 0)
                d_up = d_up + d_base * rad[t, k * width : (k + 1) * width, e : e + CH]
                der[k * width : (k + 1) * width, e : e + CH] = (d_base * up).astype(BF16)
            if t == 1:
                dlift[:, e : e + CH] = d_up.astype(BF16)
        return d_a

    def edge_rows(t, d_a):
        span = [(0, 1), (1, 4), (4, 9)]
        for e in range(0, edges, CH):
            pick = ohr[:, e : e + CH].astype(F32)
            for k, (lo, hi) in enumerate(span):
                q = dg(d_a[k], base[t, k * width : (k + 1) * width, e : e + CH], 1, 0)
                for m in range(lo, hi):
                    part = q[(m - lo) * atoms : (m - lo + 1) * atoms] * pick
                    line = jnp.sum(part, axis=0, keepdims=True)
                    if t == 1:
                        drow[m : m + 1, e : e + CH] = line
                    else:
                        drow[m : m + 1, e : e + CH] += line
        d_hidden = dg(jnp.concatenate(split(wout_ref[t]), axis=0), der[...], 1, 0)
        d_hidden = d_hidden[0:rh] + d_hidden[rh : 2 * rh]
        pre = pre_s[t]
        sig = jax.nn.sigmoid(pre)
        d_pre = d_hidden * (sig * (1.0 + pre * (1.0 - sig)))
        d_basis = dg3(win_ref[t], d_pre, 1, 0)
        gap = rows[3:4] - centres
        slope = jnp.sum(d_basis * basis_of() * gap, axis=0, keepdims=True) * (-2.0 * nb * nb)
        if t == 1:
            drow[9:10] = slope
        else:
            drow[9:10] += slope

    radial(0)
    prod1, a1_one, a2_one = pooled(0)
    h1 = h0 + dg3(prod1, wmix_ref[0], 1, 0)
    h_own[...] = h1.astype(BF16)
    second = exchange(1, lambda u: h_own, h_in, -1)
    h_in[here] = h_own[...]
    rone = jnp.broadcast_to(rone_ref[...], (8, width))
    energy1 = dg3(rone, h1, 1, 1)[0:1]
    radial(1)
    rhid = rhid_ref[...]
    mixed = dg3(rhid, wmix_ref[1], 1, 1)
    lifted_mix = dg3(wmix_ref[0], wup_ref[1], 1, 0)
    ro_own = dg3(rhid, h_own[...].astype(F32), 1, 1)
    eye = lax.broadcasted_iota(jnp.int32, (rhid.shape[0],) * 2, 0) == (
        lax.broadcasted_iota(jnp.int32, (rhid.shape[0],) * 2, 1)
    )
    rout = jnp.sum(jnp.where(eye, rout_ref[...], 0.0), axis=1, keepdims=True)
    wt_h, wt_l = split(wup_ref[1].T)
    for c in second:
        c.wait_recv()

    feats = h_in[...].reshape(ghosts, width)
    ghost_lift = (dg(wt_h, feats, 1, 1) + dg(wt_l, feats, 1, 1)).astype(BF16)
    for e in range(0, edges, CH):
        lift[1, :, e : e + CH] = dg(ghost_lift, ohs[:, e : e + CH], 1, 0)
    prod2, a1_two, a2_two = pooled(1)
    ro_pre = ro_own + dg3(mixed, prod2, 1, 1)
    ro_sig = jax.nn.sigmoid(ro_pre)
    energy2 = jnp.sum(ro_pre * ro_sig * rout, axis=0, keepdims=True)
    energy_ref[0, 0] = (energy1 + energy2) * atom_row

    d_ro = rout * atom_row * (ro_sig * (1.0 + ro_pre * (1.0 - ro_sig)))
    d_prod2 = dg3(d_ro, mixed, 0, 0)
    d_a = pulled(1, d_prod2, a1_two, a2_two)
    third = []
    for t in range(tiles):
        d_ghost = dg(ohs[t * 128 : (t + 1) * 128], dlift[...], 1, 1)
        for j in range(4):
            if 4 * t + j < total:
                dl_out[4 * t + j] = d_ghost[32 * j : 32 * j + 32].astype(BF16)
        third += exchange(2, lambda u: dl_out.at[u], dl_in, 1, t)
    dl_in[here] = dl_out[here]
    edge_rows(1, d_a)
    d_own1 = dg3(d_ro, rhid, 0, 0) + atom_col * rone_ref[...]
    d_prod1 = dg3(d_own1, wmix_ref[0], 1, 1)
    for c in third:
        c.wait_recv()

    gathered = dl_in[0].astype(F32)
    for u in range(1, total):
        gathered = gathered + dl_in[u].astype(F32)
    d_prod1 = d_prod1 + dg3(gathered, lifted_mix, 1, 1)
    d_a = pulled(0, d_prod1, a1_one, a2_one)
    edge_rows(0, d_a)

    x, y, z, inner = rows[0:1], rows[1:2], rows[2:3], rows[4:5]
    env8 = inner * inner * (1.0 / mean_degree)
    d_env = drow[0:1] * rows[8:9]
    for m in range(1, 9):
        d_env = d_env + drow[m : m + 1] * rows[8 + m : 9 + m]
    d_dist = 2.0 * (drow[9:10] - 2.0 * d_env * inner)
    dh = [drow[m : m + 1] * env8 for m in range(9)]
    d_x = d_dist * x + s3 * dh[1] + s15 * (y * dh[4] + z * dh[6] + x * dh[7]) - s5 * x * dh[8]
    d_y = d_dist * y + s3 * dh[2] + s15 * (x * dh[4] + z * dh[5] - y * dh[7]) - s5 * y * dh[8]
    d_z = d_dist * z + s3 * dh[3] + s15 * (y * dh[5] + x * dh[6]) + 2.0 * s5 * z * dh[8]
    drow[0:1] = d_x / cutoff_radius
    drow[1:2] = d_y / cutoff_radius
    drow[2:3] = d_z / cutoff_radius
    drow[3:8] = jnp.zeros((5, edges), F32)
    d_rel = drow[0:8]
    d_hi = d_rel.astype(BF16).astype(F32)
    both = jnp.concatenate([d_hi, d_rel - d_hi], axis=0).astype(BF16)
    fourth = []
    for t in range(tiles):
        back = dg(both, ohs[t * 128 : (t + 1) * 128], 1, 1)
        dp_out[t] = back[0:8] + back[8:16]
        fourth += exchange(3, lambda u: dp_out.at[u // 4], dp_in, 1, t)
    dp_in[here] = dp_out[here // 4]
    own = dg(both, ohr[...], 1, 1)
    for c in first + second + third:
        c.wait_send()
    for c in fourth:
        c.wait_recv()
    fold = jnp.zeros((8, 128), F32)
    for u in range(total):
        j = u % 4
        inside = (lane >= 32 * j) & (lane < 32 * j + 32)
        fold = fold + jnp.where(inside, dp_in[u], 0.0)
    fold = fold + pltpu.roll(fold, 64, 1)
    fold = fold + pltpu.roll(fold, 32, 1)
    force = own[0:8] + own[8:16] - fold[:, 0:atoms]
    for a in range(3):
        force_ref[a, 0, 0] = force[a : a + 1]
    for c in fourth:
        c.wait_send()


def local(
    sizes,
    positions,
    species,
    atom_count,
    edge_count,
    sender,
    receiver,
    image_shift,
    embed,
    radial_in,
    radial_out,
    w_up,
    lam,
    w_mix,
    read_one,
    read_hidden,
    read_out,
):
    atoms = positions.shape[-1]
    edges = sender.shape[-1]
    nspec, width = embed.shape
    rh = radial_in.shape[2]
    total = len(offsets_of(sizes))
    tiles = (total + 3) // 4
    ghosts = tiles * 128
    operands = (
        positions,
        species,
        atom_count,
        edge_count,
        sender,
        receiver,
        image_shift,
        embed,
        radial_in,
        radial_out,
        w_up,
        lam,
        w_mix,
        read_one.reshape(1, width),
        read_hidden.T,
        read_out.reshape(1, -1),
    )
    vmem = pl.BlockSpec(memory_space=pltpu.VMEM)
    energy, force = pl.pallas_call(
        functools.partial(kernel, sizes),
        out_shape=(
            jax.ShapeDtypeStruct((1, 1, 1, atoms), F32),
            jax.ShapeDtypeStruct((3, 1, 1, 1, atoms), F32),
        ),
        in_specs=[pl.BlockSpec(memory_space=pltpu.HBM)] * INPUTS,
        out_specs=(vmem, vmem),
        scratch_shapes=[pltpu.VMEM(a.shape, a.dtype) for a in operands]
        + [
            pltpu.VMEM((8, 128), F32),
            pltpu.VMEM((total, 8, 128), F32),
            pltpu.VMEM((atoms, width), BF16),
            pltpu.VMEM((4 * tiles, atoms, width), BF16),
            pltpu.VMEM((total, atoms, width), BF16),
            pltpu.VMEM((total, atoms, width), BF16),
            pltpu.VMEM((tiles, 8, 128), F32),
            pltpu.VMEM((total, 8, 128), F32),
            pltpu.VMEM(((nspec + 15) // 16 * 16, width), F32),
            pltpu.VMEM((ghosts, edges), BF16),
            pltpu.VMEM((atoms, edges), BF16),
            pltpu.VMEM((9 * atoms, edges), BF16),
            pltpu.VMEM((2, 3 * width, edges), F32),
            pltpu.VMEM((2, width, edges), F32),
            pltpu.VMEM((2, 3 * width, edges), BF16),
            pltpu.VMEM((2, rh, edges), F32),
            pltpu.VMEM((3 * width, edges), BF16),
            pltpu.VMEM((width, edges), BF16),
            pltpu.VMEM((24, edges), F32),
            pltpu.VMEM((16, edges), F32),
            pltpu.SemaphoreType.DMA((INPUTS,)),
            pltpu.SemaphoreType.DMA((4, total)),
            pltpu.SemaphoreType.DMA((4, total)),
        ],
        compiler_params=pltpu.CompilerParams(
            collective_id=0, has_side_effects=True, vmem_limit_bytes=64 * 1024 * 1024
        ),
    )(*operands)
    return energy, force


def solution(mesh):
    sizes = tuple(mesh.shape[a] for a in ("gx", "gy", "gz"))
    in_specs = (
        P(None, "gx", "gy", "gz", None),
        P("gx", "gy", "gz", None),
        P("gx", "gy", "gz"),
        P("gx", "gy", "gz"),
        P("gx", "gy", "gz", None),
        P("gx", "gy", "gz", None),
        P(None, "gx", "gy", "gz", None),
        P(),
        P(),
        P(),
        P(),
        P(),
        P(),
        P(),
        P(),
        P(),
    )
    out_specs = (P("gx", "gy", "gz", None), P(None, "gx", "gy", "gz", None))
    return jax.shard_map(
        functools.partial(local, sizes),
        mesh=mesh,
        in_specs=in_specs,
        out_specs=out_specs,
        check_vma=False,
    )
```

```python
import functools
import itertools

import jax
import jax.numpy as jnp
from jax import lax
from jax.experimental import pallas as pl
from jax.experimental.pallas import tpu as pltpu
from jax.sharding import PartitionSpec as P

cutoff_radius = 5.0
lattice_step = 2.25
mean_degree = 8.0
F32 = jnp.float32
BF16 = jnp.bfloat16
MESH = pl.DeviceIdType.MESH
CH = 256
INPUTS = 16


def dg(a, b, ca, cb):
    return lax.dot_general(a, b, (((ca,), (cb,)), ((), ())), preferred_element_type=F32)


def split(x):
    hi = x.astype(BF16)
    return hi, (x - hi.astype(F32)).astype(BF16)


def dg3(a, b, ca, cb):
    ah, al = split(a)
    bh, bl = split(b)
    return dg(ah, bh, ca, cb) + (dg(ah, bl, ca, cb) + dg(al, bh, ca, cb))


def parts(x):
    p1 = x.astype(BF16).astype(F32)
    p2 = (x - p1).astype(BF16).astype(F32)
    p3 = x - p1 - p2
    return jnp.concatenate([p1, p2, p3, jnp.zeros_like(x)], axis=0).astype(BF16)


def whole(y):
    return y[0:8] + y[8:16] + y[16:24]


def offsets_of(sizes):
    per_axis = [(-1, 0, 1) if n >= 3 else (-1, 0) if n == 2 else (0,) for n in sizes]
    return list(itertools.product(*per_axis))


def kernel(
    sizes,
    *refs,
):
    hbm = refs[:INPUTS]
    energy_ref, force_ref = refs[INPUTS : INPUTS + 2]
    held = refs[INPUTS + 2 : 2 * INPUTS + 2]
    body(sizes, hbm, energy_ref, force_ref, held, *refs[2 * INPUTS + 2 :])


def body(
    sizes,
    hbm,
    energy_ref,
    force_ref,
    held,
    own8,
    gpos_in,
    h_own,
    h_in,
    dl_out,
    dl_in,
    dp_out,
    dp_in,
    emb_s,
    ohs,
    ohr,
    pool,
    rad,
    lift,
    base,
    pre_s,
    der,
    dlift,
    rows,
    drow,
    in_sem,
    send_sem,
    recv_sem,
):
    (
        pos_ref,
        spec_ref,
        acount_ref,
        ecount_ref,
        sender_ref,
        receiver_ref,
        shift_ref,
        embed_ref,
        win_ref,
        wout_ref,
        wup_ref,
        lam_ref,
        wmix_ref,
        rone_ref,
        rhid_ref,
        rout_ref,
    ) = held
    fetch = [
        pltpu.make_async_copy(src, dst, in_sem.at[i])
        for i, (src, dst) in enumerate(zip(hbm, held))
    ]
    atoms = pos_ref.shape[-1]
    edges = sender_ref.shape[-1]
    nb = win_ref.shape[1]
    rh = win_ref.shape[2]
    width = embed_ref.shape[1]
    nspec = embed_ref.shape[0]
    spad = emb_s.shape[0]
    offs = offsets_of(sizes)
    total = len(offs)
    tiles = dp_out.shape[0]
    ghosts = tiles * 128
    here = offs.index(tuple(0 for _ in sizes))
    me = [lax.axis_index(a) for a in ("gx", "gy", "gz")]

    def device(off, sign):
        return tuple(
            lax.rem(m + (sign * o) % n, n) if o else m for m, o, n in zip(me, off, sizes)
        )

    others = [u for u in range(total) if u != here]
    others.sort(key=lambda u: -sum(o != 0 for o in offs[u]))

    barrier = pltpu.get_barrier_semaphore()
    for u in others:
        pl.semaphore_signal(barrier, inc=1, device_id=device(offs[u], 1), device_id_type=MESH)
    for c in fetch:
        c.start()

    own8[...] = jnp.zeros_like(own8)
    fetch[0].wait()
    fetch[1].wait()
    mine = jnp.concatenate(
        [pos_ref[a, 0, 0] for a in range(3)] + [spec_ref[0, 0].astype(F32)], axis=0
    )
    own8[0:4, :] = jnp.concatenate([mine] * 4, axis=1)
    pl.semaphore_wait(barrier, len(others))

    def copy(phase, u, src, dst, sign):
        return pltpu.make_async_remote_copy(
            src_ref=src,
            dst_ref=dst,
            send_sem=send_sem.at[phase, u],
            recv_sem=recv_sem.at[phase, u],
            device_id=device(offs[u], sign),
            device_id_type=MESH,
        )

    def exchange(phase, source, target, sign, tile=None):
        started = [
            copy(phase, u, source(u), target.at[u], sign)
            for u in others
            if tile is None or u // 4 == tile
        ]
        for c in started:
            c.start()
        return started

    first = exchange(0, lambda u: own8, gpos_in, -1)

    gpos_in[here] = own8[...]
    for c in fetch[2:]:
        c.wait()
    send_id = sender_ref[0, 0]
    block = jnp.right_shift(send_id, 5)
    slot = send_id - block * 32
    bx = (block >= 9).astype(jnp.int32) + (block >= 18).astype(jnp.int32)
    rest = block - 9 * bx
    by = (rest >= 3).astype(jnp.int32) + (rest >= 6).astype(jnp.int32)
    bz = rest - 3 * by
    flat = jnp.zeros_like(block)
    for d, n in zip((bx, by, bz), sizes):
        if n >= 3:
            flat = flat * 3 + d
        elif n == 2:
            flat = flat * 2 + jnp.where(d == 1, 1, 0)
    ghost_id = flat * 32 + slot
    sub = lax.broadcasted_iota(jnp.int32, (128, CH), 0)
    for e in range(0, edges, CH):
        for t in range(tiles):
            ohs[t * 128 : (t + 1) * 128, e : e + CH] = jnp.where(
                sub == ghost_id[:, e : e + CH] - t * 128, 1.0, 0.0
            ).astype(BF16)
    recv_id = receiver_ref[0, 0]
    near = lax.broadcasted_iota(jnp.int32, (atoms, edges), 0) == recv_id
    ohr[...] = jnp.where(near, 1.0, 0.0).astype(BF16)
    at_recv = whole(dg(parts(own8[...])[:, 0:atoms], ohr[...], 1, 0))
    emb_s[...] = jnp.zeros_like(emb_s)
    emb_s[0:nspec, :] = embed_ref[...]
    emb = emb_s[...].astype(BF16)
    wu_h, wu_l = split(wup_ref[0])
    table = (dg(emb, wu_h, 1, 0) + dg(emb, wu_l, 1, 0)).astype(BF16)
    kind = lax.broadcasted_iota(jnp.int32, (spad, 128), 0).astype(F32)
    own_kind = jnp.where(kind == own8[3:4, :], 1.0, 0.0).astype(BF16)
    h0 = dg(own_kind, emb, 0, 0)[0:atoms]
    valid = lax.broadcasted_iota(jnp.int32, (1, edges), 1) < ecount_ref[0]
    atom_row = (lax.broadcasted_iota(jnp.int32, (1, atoms), 1) < acount_ref[0]).astype(F32)
    atom_col = (lax.broadcasted_iota(jnp.int32, (atoms, width), 0) < acount_ref[0]).astype(F32)
    if h_in.shape[0] > total:
        h_in[total:] = jnp.zeros((h_in.shape[0] - total, atoms, width), BF16)

    for c in first:
        c.wait_recv()

    lane = lax.broadcasted_iota(jnp.int32, (8, 128), 1)
    cols = []
    for t in range(tiles):
        tile = jnp.zeros((8, 128), F32)
        for j in range(4):
            if 4 * t + j < total:
                inside = (lane >= 32 * j) & (lane < 32 * j + 32)
                tile = jnp.where(inside, gpos_in[4 * t + j], tile)
        cols.append(tile)
    gpos = jnp.concatenate(cols, axis=1)
    gkind = jnp.concatenate(
        [jnp.where(kind == c[3:4, :], 1.0, 0.0).astype(BF16) for c in cols], axis=1
    )
    ghost_lift = dg(table, gkind, 0, 0).astype(BF16)
    lhs = jnp.concatenate([ghost_lift, parts(gpos)], axis=0)
    at_send = []
    for e in range(0, edges, CH):
        got = dg(lhs, ohs[:, e : e + CH], 1, 0)
        lift[0, :, e : e + CH] = got[0:width]
        at_send.append(whole(got[width:]))
    at_send = jnp.concatenate(at_send, axis=1)

    def axis(a, n, cells):
        length = n * cells * lattice_step
        moved = at_send[a : a + 1] + shift_ref[a, 0, 0].astype(F32) * length
        return (moved - at_recv[a : a + 1]) / cutoff_radius

    x = axis(0, sizes[0], 4)
    y = axis(1, sizes[1], 4)
    z = axis(2, sizes[2], atoms // 16)
    dist2 = x * x + y * y + z * z
    inner = jnp.where(valid, jnp.maximum(1.0 - dist2, 0.0), 0.0)
    env = inner * inner
    s3, s5, s15 = 3.0**0.5, 5.0**0.5, 15.0**0.5
    harm = [
        jnp.ones_like(x),
        s3 * x,
        s3 * y,
        s3 * z,
        s15 * x * y,
        s15 * y * z,
        s15 * x * z,
        0.5 * s15 * (x * x - y * y),
        0.5 * s5 * (2.0 * z * z - x * x - y * y),
    ]
    rows[0:1] = x
    rows[1:2] = y
    rows[2:3] = z
    rows[3:4] = dist2
    rows[4:5] = inner
    for m in range(9):
        rows[8 + m : 9 + m] = harm[m] * (1.0 / mean_degree)
        weight = harm[m] * env * (1.0 / mean_degree)
        pool[atoms * m : atoms * (m + 1), :] = jnp.where(near, weight, 0.0).astype(BF16)

    centres = lax.broadcasted_iota(jnp.int32, (nb, edges), 0).astype(F32) / (nb - 1)

    def basis_of():
        return jnp.exp(-jnp.square((rows[3:4] - centres) * nb))

    def radial(t):
        basis = basis_of()
        bh = basis.astype(BF16).astype(F32)
        bl = basis - bh
        wi = win_ref[t]
        wh = wi.astype(BF16).astype(F32)
        wl = wi - wh
        pre = dg(
            jnp.concatenate([wh, wh, wl, wl], axis=0).astype(BF16),
            jnp.concatenate([bh, bl, bh, bl], axis=0).astype(BF16),
            0,
            0,
        )
        pre_s[t] = pre
        hidden = pre * jax.nn.sigmoid(pre)
        hh, hl = split(hidden)
        wo = wout_ref[t]
        oh = wo.astype(BF16).astype(F32)
        left = jnp.concatenate([oh, oh, wo - oh], axis=0).T.astype(BF16)
        right = jnp.concatenate([hh, hl, hh], axis=0)
        for e in range(0, edges, CH):
            rad[t, :, e : e + CH] = dg(left, right[:, e : e + CH], 1, 0)

    def pooled(t):
        for e in range(0, edges, CH):
            up = lift[t, :, e : e + CH]
            for k in range(3):
                base[t, k * width : (k + 1) * width, e : e + CH] = (
                    rad[t, k * width : (k + 1) * width, e : e + CH] * up
                ).astype(BF16)
        a0 = dg(pool[0:atoms], base[t, 0:width], 1, 1)
        a1 = dg(pool[atoms : 4 * atoms], base[t, width : 2 * width], 1, 1)
        a2 = dg(pool[4 * atoms : 9 * atoms], base[t, 2 * width : 3 * width], 1, 1)
        a1 = [a1[atoms * m : atoms * (m + 1)] for m in range(3)]
        a2 = [a2[atoms * m : atoms * (m + 1)] for m in range(5)]
        l0, l1 = lam_ref[t, 0:1], lam_ref[t, 1:2]
        q1 = sum(a * a for a in a1)
        q2 = sum(a * a for a in a2)
        return a0 + l0 * q1 + l1 * q2, a1, a2

    def pulled(t, d_prod, a1, a2):
        l0, l1 = lam_ref[t, 0:1], lam_ref[t, 1:2]
        g1 = 2.0 * l0 * d_prod
        g2 = 2.0 * l1 * d_prod
        d_a = [
            d_prod,
            jnp.concatenate([g1 * a for a in a1], axis=0),
            jnp.concatenate([g2 * a for a in a2], axis=0),
        ]
        d_t = [d.T.astype(BF16) for d in d_a]
        d_a = [d.astype(BF16) for d in d_a]
        for e in range(0, edges, CH):
            if t == 1:
                d_up = jnp.zeros((width, CH), F32)
                for k in range(3):
                    piece = rad[t, k * width : (k + 1) * width, e : e + CH]
                    d_up = d_up + d_base_of(d_t, k, e) * piece
                dlift[:, e : e + CH] = d_up.astype(BF16)
        return d_a, d_t

    def d_base_of(d_t, k, e):
        lo, hi = ((0, 1), (1, 4), (4, 9))[k]
        return dg(d_t[k], pool[lo * atoms : hi * atoms, e : e + CH], 1, 0)

    def radial_pulled(t, d_t):
        for e in range(0, edges, CH):
            up = lift[t, :, e : e + CH]
            for k in range(3):
                der[k * width : (k + 1) * width, e : e + CH] = (
                    d_base_of(d_t, k, e) * up
                ).astype(BF16)

    def edge_rows(t, d_a):
        span = [(0, 1), (1, 4), (4, 9)]
        for e in range(0, edges, CH):
            pick = ohr[:, e : e + CH].astype(F32)
            for k, (lo, hi) in enumerate(span):
                q = dg(d_a[k], base[t, k * width : (k + 1) * width, e : e + CH], 1, 0)
                for m in range(lo, hi):
                    part = q[(m - lo) * atoms : (m - lo + 1) * atoms] * pick
                    line = jnp.sum(part, axis=0, keepdims=True)
                    if t == 1:
                        drow[m : m + 1, e : e + CH] = line
                    else:
                        drow[m : m + 1, e : e + CH] += line
        d_hidden = dg(jnp.concatenate(split(wout_ref[t]), axis=0), der[...], 1, 0)
        d_hidden = d_hidden[0:rh] + d_hidden[rh : 2 * rh]
        pre = pre_s[t]
        sig = jax.nn.sigmoid(pre)
        d_pre = d_hidden * (sig * (1.0 + pre * (1.0 - sig)))
        d_basis = dg3(win_ref[t], d_pre, 1, 0)
        gap = rows[3:4] - centres
        slope = jnp.sum(d_basis * basis_of() * gap, axis=0, keepdims=True) * (-2.0 * nb * nb)
        if t == 1:
            drow[9:10] = slope
        else:
            drow[9:10] += slope

    radial(0)
    prod1, a1_one, a2_one = pooled(0)
    h1 = h0 + dg3(prod1, wmix_ref[0], 1, 0)
    h_own[...] = h1.astype(BF16)
    second = exchange(1, lambda u: h_own, h_in, -1)
    h_in[here] = h_own[...]
    rone = jnp.broadcast_to(rone_ref[...], (8, width))
    energy1 = dg3(rone, h1, 1, 1)[0:1]
    radial(1)
    rhid = rhid_ref[...]
    mixed = dg3(rhid, wmix_ref[1], 1, 1)
    lifted_mix = dg3(wmix_ref[0], wup_ref[1], 1, 0)
    ro_own = dg3(rhid, h_own[...].astype(F32), 1, 1)
    eye = lax.broadcasted_iota(jnp.int32, (rhid.shape[0],) * 2, 0) == (
        lax.broadcasted_iota(jnp.int32, (rhid.shape[0],) * 2, 1)
    )
    rout = jnp.sum(jnp.where(eye, rout_ref[...], 0.0), axis=1, keepdims=True)
    wt_h, wt_l = split(wup_ref[1].T)
    for c in second:
        c.wait_recv()

    feats = h_in[...].reshape(ghosts, width)
    ghost_lift = (dg(wt_h, feats, 1, 1) + dg(wt_l, feats, 1, 1)).astype(BF16)
    for e in range(0, edges, CH):
        lift[1, :, e : e + CH] = dg(ghost_lift, ohs[:, e : e + CH], 1, 0)
    prod2, a1_two, a2_two = pooled(1)
    ro_pre = ro_own + dg3(mixed, prod2, 1, 1)
    ro_sig = jax.nn.sigmoid(ro_pre)
    energy2 = jnp.sum(ro_pre * ro_sig * rout, axis=0, keepdims=True)
    energy_ref[0, 0] = (energy1 + energy2) * atom_row

    d_ro = rout * atom_row * (ro_sig * (1.0 + ro_pre * (1.0 - ro_sig)))
    d_prod2 = dg3(d_ro, mixed, 0, 0)
    d_a, d_t = pulled(1, d_prod2, a1_two, a2_two)
    third = []
    for t in range(tiles):
        d_ghost = dg(ohs[t * 128 : (t + 1) * 128], dlift[...], 1, 1)
        for j in range(4):
            if 4 * t + j < total:
                dl_out[4 * t + j] = d_ghost[32 * j : 32 * j + 32].astype(BF16)
        third += exchange(2, lambda u: dl_out.at[u], dl_in, 1, t)
    dl_in[here] = dl_out[here]
    radial_pulled(1, d_t)
    edge_rows(1, d_a)
    d_own1 = dg3(d_ro, rhid, 0, 0) + atom_col * rone_ref[...]
    d_prod1 = dg3(d_own1, wmix_ref[0], 1, 1)
    for c in third:
        c.wait_recv()

    gathered = dl_in[0].astype(F32)
    for u in range(1, total):
        gathered = gathered + dl_in[u].astype(F32)
    d_prod1 = d_prod1 + dg3(gathered, lifted_mix, 1, 1)
    d_a, d_t = pulled(0, d_prod1, a1_one, a2_one)
    radial_pulled(0, d_t)
    edge_rows(0, d_a)

    x, y, z, inner = rows[0:1], rows[1:2], rows[2:3], rows[4:5]
    env8 = inner * inner * (1.0 / mean_degree)
    d_env = drow[0:1] * rows[8:9]
    for m in range(1, 9):
        d_env = d_env + drow[m : m + 1] * rows[8 + m : 9 + m]
    d_dist = 2.0 * (drow[9:10] - 2.0 * d_env * inner)
    dh = [drow[m : m + 1] * env8 for m in range(9)]
    d_x = d_dist * x + s3 * dh[1] + s15 * (y * dh[4] + z * dh[6] + x * dh[7]) - s5 * x * dh[8]
    d_y = d_dist * y + s3 * dh[2] + s15 * (x * dh[4] + z * dh[5] - y * dh[7]) - s5 * y * dh[8]
    d_z = d_dist * z + s3 * dh[3] + s15 * (y * dh[5] + x * dh[6]) + 2.0 * s5 * z * dh[8]
    drow[0:1] = d_x / cutoff_radius
    drow[1:2] = d_y / cutoff_radius
    drow[2:3] = d_z / cutoff_radius
    drow[3:8] = jnp.zeros((5, edges), F32)
    d_rel = drow[0:8]
    d_hi = d_rel.astype(BF16).astype(F32)
    both = jnp.concatenate([d_hi, d_rel - d_hi], axis=0).astype(BF16)
    fourth = []
    for t in range(tiles):
        back = dg(both, ohs[t * 128 : (t + 1) * 128], 1, 1)
        dp_out[t] = back[0:8] + back[8:16]
        fourth += exchange(3, lambda u: dp_out.at[u // 4], dp_in, 1, t)
    dp_in[here] = dp_out[here // 4]
    own = dg(both, ohr[...], 1, 1)
    for c in first + second + third:
        c.wait_send()
    for c in fourth:
        c.wait_recv()
    fold = jnp.zeros((8, 128), F32)
    for u in range(total):
        j = u % 4
        inside = (lane >= 32 * j) & (lane < 32 * j + 32)
        fold = fold + jnp.where(inside, dp_in[u], 0.0)
    fold = fold + pltpu.roll(fold, 64, 1)
    fold = fold + pltpu.roll(fold, 32, 1)
    force = own[0:8] + own[8:16] - fold[:, 0:atoms]
    for a in range(3):
        force_ref[a, 0, 0] = force[a : a + 1]
    for c in fourth:
        c.wait_send()


def local(
    sizes,
    positions,
    species,
    atom_count,
    edge_count,
    sender,
    receiver,
    image_shift,
    embed,
    radial_in,
    radial_out,
    w_up,
    lam,
    w_mix,
    read_one,
    read_hidden,
    read_out,
):
    atoms = positions.shape[-1]
    edges = sender.shape[-1]
    nspec, width = embed.shape
    rh = radial_in.shape[2]
    total = len(offsets_of(sizes))
    tiles = (total + 3) // 4
    ghosts = tiles * 128
    operands = (
        positions,
        species,
        atom_count,
        edge_count,
        sender,
        receiver,
        image_shift,
        embed,
        radial_in,
        radial_out,
        w_up,
        lam,
        w_mix,
        read_one.reshape(1, width),
        read_hidden.T,
        read_out.reshape(1, -1),
    )
    vmem = pl.BlockSpec(memory_space=pltpu.VMEM)
    energy, force = pl.pallas_call(
        functools.partial(kernel, sizes),
        out_shape=(
            jax.ShapeDtypeStruct((1, 1, 1, atoms), F32),
            jax.ShapeDtypeStruct((3, 1, 1, 1, atoms), F32),
        ),
        in_specs=[pl.BlockSpec(memory_space=pltpu.HBM)] * INPUTS,
        out_specs=(vmem, vmem),
        scratch_shapes=[pltpu.VMEM(a.shape, a.dtype) for a in operands]
        + [
            pltpu.VMEM((8, 128), F32),
            pltpu.VMEM((total, 8, 128), F32),
            pltpu.VMEM((atoms, width), BF16),
            pltpu.VMEM((4 * tiles, atoms, width), BF16),
            pltpu.VMEM((total, atoms, width), BF16),
            pltpu.VMEM((total, atoms, width), BF16),
            pltpu.VMEM((tiles, 8, 128), F32),
            pltpu.VMEM((total, 8, 128), F32),
            pltpu.VMEM(((nspec + 15) // 16 * 16, width), F32),
            pltpu.VMEM((ghosts, edges), BF16),
            pltpu.VMEM((atoms, edges), BF16),
            pltpu.VMEM((9 * atoms, edges), BF16),
            pltpu.VMEM((2, 3 * width, edges), F32),
            pltpu.VMEM((2, width, edges), F32),
            pltpu.VMEM((2, 3 * width, edges), BF16),
            pltpu.VMEM((2, rh, edges), F32),
            pltpu.VMEM((3 * width, edges), BF16),
            pltpu.VMEM((width, edges), BF16),
            pltpu.VMEM((24, edges), F32),
            pltpu.VMEM((16, edges), F32),
            pltpu.SemaphoreType.DMA((INPUTS,)),
            pltpu.SemaphoreType.DMA((4, total)),
            pltpu.SemaphoreType.DMA((4, total)),
        ],
        compiler_params=pltpu.CompilerParams(
            collective_id=0, has_side_effects=True, vmem_limit_bytes=64 * 1024 * 1024
        ),
    )(*operands)
    return energy, force


def solution(mesh):
    sizes = tuple(mesh.shape[a] for a in ("gx", "gy", "gz"))
    in_specs = (
        P(None, "gx", "gy", "gz", None),
        P("gx", "gy", "gz", None),
        P("gx", "gy", "gz"),
        P("gx", "gy", "gz"),
        P("gx", "gy", "gz", None),
        P("gx", "gy", "gz", None),
        P(None, "gx", "gy", "gz", None),
        P(),
        P(),
        P(),
        P(),
        P(),
        P(),
        P(),
        P(),
        P(),
    )
    out_specs = (P("gx", "gy", "gz", None), P(None, "gx", "gy", "gz", None))
    return jax.shard_map(
        functools.partial(local, sizes),
        mesh=mesh,
        in_specs=in_specs,
        out_specs=out_specs,
        check_vma=False,
    )
```
